512 devices in a mesh: ctx: 64 (over x, z), head: 8 (over y, core).
Axes of the slice: x: 4, y: 4, z: 16, core: 2. Of those that a mesh axis runs over, the one named last changes fastest.
Arguments:
- queries: bfloat16 [65536, 4096], P(('ctx', 'head')), may hold values from -6 to 6
- keys: bfloat16 [65536, 1024], P(('ctx', 'head')), may hold values from -6 to 6
- values: bfloat16 [65536, 1024], P(('ctx', 'head')), may hold values from -6 to 6
- doc_ids: int32 [65536], P('ctx'), may hold values from 0 to 127, never falling along the last dimension, each value on 1 to 1024 neighbouring positions
- sample_rows: int32 [4096], P('ctx'), may hold values from 0 to 1023, as said below
- owners: int32 [4096, 1], P('ctx'), may hold values from 0 to 63; in each aligned block of 64 rows (0 to 63, 64 to 127, ...) at most 2 rows name the same one
- targets: int32 [4096, 2], P('ctx'), may hold values from 0 to 2047
- in_proj: bfloat16 [4096, 1024], P('head'), may hold values from -0.09375 to 0.09375
- dec_gain: float32 [1024], replicated, may hold values from 0.5 to 1.5
- code_heads: bfloat16 [2, 1024, 2048], P(None, None, 'head'), may hold values from -32 to 32
Outputs:
- attended: bfloat16 [65536, 4096], P('ctx', 'head')
- slot_loss: float32 [64, 128], P('ctx')
The draws below stay inside these ranges and needn't reach their ends.
Inputs may be any that keep to these rules, and one draw needn't show every extreme that they name: `sample_rows`: entry j of one ctx index's list lies in the j-th aligned group of 16 frames of its block. `owners`: within the 64 entries of one ctx index at most 2 name one owner. `doc_ids`: never falling; each document 1 to 1024 frames, one exactly 1024.
All inputs are finite; a program needn't handle non-finite values.
Results may differ from the reference program's by a relative error of at most 0.0036.
Values may be sent and summed in bfloat16 or wider, within the bound.
No kernel may reach another device: no remote copies, remote signals or barrier semaphores. Data moves between devices by JAX's collectives and lax.ppermute only.
A program may use at most 64 MiB of HBM per device.

```python
import math
import jax
import jax.numpy as jnp
import numpy as np
from jax import lax

QUERY_HEADS = 32
KEY_VALUE_HEADS = 8
HEAD_SIZE = 128
DD = 1024
CODES = 2048
CB = 2
BLOCK_FRAMES = 1024
TOTAL_FRAMES = 65536
SAMP = 64
SAMPLED = 4096
CAP = 2
N_CTX = 64


def base_field_rows(key, columns):
    return jnp.clip(jax.random.normal(key, (TOTAL_FRAMES, columns), jnp.float32), -6.0, 6.0)


def draw_queries(key, part):
    key = jax.random.fold_in(key, 1)
    return base_field_rows(key, QUERY_HEADS * HEAD_SIZE).astype(jnp.bfloat16)


def draw_keys(key, part):
    key = jax.random.fold_in(key, 2)
    return base_field_rows(key, KEY_VALUE_HEADS * HEAD_SIZE).astype(jnp.bfloat16)


def draw_sample_rows(key, part):
    key = jax.random.fold_in(key, 3)
    entry = jnp.arange(SAMPLED, dtype=jnp.int32)
    return 16 * (entry % SAMP) + jax.random.randint(key, (SAMPLED,), 0, 16, jnp.int32)


def draw_code_heads(key, part):
    key = jax.random.fold_in(key, 4)
    first = jax.random.fold_in(key, 0)
    normal_part = jax.random.normal(first, (CB, DD, CODES), jnp.float32) / jnp.sqrt(jnp.float32(DD))
    return jnp.clip(3.0 * normal_part, -32.0, 32.0).astype(jnp.bfloat16)


def place_ends(drawn, stream_key, low, largest):
    place = [jax.random.randint(jax.random.fold_in(stream_key, axis), (), 0, length) for axis, length in enumerate(drawn.shape)]
    longest = drawn.shape.index(max(drawn.shape))
    next_to = place[:longest] + [(place[longest] + 1) % drawn.shape[longest]] + place[longest + 1:]
    return drawn.at[tuple(place)].set(low).at[tuple(next_to)].set(largest)


def level_of(rng, shape, shards, low, high):
    factor_of = 1.0
    for position, blocks in shards:
        heights = jax.random.uniform(jax.random.fold_in(jax.random.fold_in(rng, 6), position), (blocks,), jnp.float32, low / len(shards), high / len(shards))
        factor_of = factor_of * jnp.repeat(jnp.exp(heights), shape[position] // blocks).reshape((-1,) + (1,) * (len(shape) - 1 - position))
    return factor_of


def split_up(amount, total, limit, skew):
    weights = [(1 << 20) // math.isqrt(rank ** skew) + 1 for rank in range(2, amount + 1)]
    spare, holding = total - limit - (amount - 1), [1] * (amount - 1)
    while spare > 0:
        free = [i for i in range(amount - 1) if holding[i] < limit]
        mass, remaining = sum([weights[i] for i in free]), spare
        for i in free:
            extra = min(limit - holding[i], max(1, remaining * weights[i] // mass), spare)
            holding[i] = holding[i] + extra
            spare = spare - extra
    return np.array([limit] + holding)


def ragged_sizes(stream_key, number_of, total, most, skew):
    if number_of == 2:
        one = jax.random.randint(stream_key, (), max(1, total - most), min(most, total - 1) + 1)
        return jnp.stack([one, total - one])
    sizes = jnp.asarray(split_up(number_of, total, most, skew), jnp.int32)
    twos = (number_of - 1) // 2
    source_of, receiver = sizes[1:1 + 2 * twos:2], sizes[2:2 + 2 * twos:2]
    room = jnp.minimum(source_of - 1, most - receiver)
    passed = jax.random.randint(jax.random.fold_in(stream_key, 1), (twos,), 0, 1 << 20) % (room + 1)
    sizes = sizes.at[1:1 + 2 * twos:2].set(source_of - passed).at[2:2 + 2 * twos:2].set(receiver + passed)
    return sizes[jax.random.permutation(jax.random.fold_in(stream_key, 2), number_of)]


def routed_block(rng, own, number, rows, count, top, most, lean):
    ranking = jax.random.permutation(rng, count)
    crowded, ordinary = load_shares(count, rows * top, most, lean, True), load_shares(count, rows * top, most, lean, False)
    places = jnp.arange(count)

    def named(lengths, offset_by):
        used = int((lengths > 0).sum())
        fixed = max(1, used // 4)
        passed = fixed + (places - fixed + offset_by * (used - fixed)) % max(1, count - fixed)
        return jnp.zeros((count,), jnp.int32).at[ranking[jnp.where(places < fixed, places, passed)]].set(jnp.asarray(lengths, jnp.int32))

    lengths = jnp.where(number % 4 == 0, named(crowded, number // 4), named(ordinary, number - number // 4 - 1))
    mixed = jax.random.permutation(jax.random.fold_in(own, 3), count)
    giver, taker = mixed[0:count // 2 * 2:2], mixed[1:count // 2 * 2:2]
    slack = jnp.minimum(lengths[giver] - 1, most - lengths[taker]) // 2
    slack = jnp.where((giver == ranking[0]) | (taker == ranking[0]) | (lengths[taker] == 0), 0, jnp.maximum(slack, 0))
    passed = jax.random.randint(jax.random.fold_in(own, 4), (count // 2,), 0, 1 << 20) % (slack + 1)
    lengths = lengths.at[giver].add(-passed).at[taker].add(passed)
    items = jnp.searchsorted(jnp.cumsum(lengths), jnp.arange(rows * top), side="right").astype(jnp.int32)
    grid = items.reshape(top, rows).T
    grid = grid[jax.random.permutation(jax.random.fold_in(own, 1), rows)]
    offset_by = jax.random.randint(jax.random.fold_in(own, 2), (rows, 1), 0, top)
    return jnp.take_along_axis(grid, (jnp.arange(top)[None, :] + offset_by) % top, axis=1)


def load_shares(number_of, total, limit, slope, full):
    loads = [(1 << 20) // math.isqrt(grade ** slope) + 1 for grade in range(1, number_of + 1)]
    largest = limit if full else min(limit, max(-(-total // number_of), total * loads[0] // sum(loads)))
    least = 1 if total - largest >= number_of - 1 else 0
    given, rest = [largest] + [least] * (number_of - 1), total - largest - least * (number_of - 1)
    while rest > 0:
        movable = [i for i in range(1, number_of) if given[i] < largest] or [i for i in range(1, number_of) if given[i] < limit]
        mass, left = sum([loads[i] for i in movable]), rest
        for i in movable:
            more = min(limit - given[i], max(1, left * loads[i] // mass), rest)
            given[i] = given[i] + more
            rest = rest - more
    return np.array(given)


def centred(own_key, shape, width, most, cuts=(), kind=jnp.bfloat16):
    drawn = jax.random.normal(own_key, shape, jnp.float32) * width
    if len(cuts) > 0:
        drawn = level_of(own_key, shape, cuts, -0.22, 0.18) * drawn
    return jnp.clip(drawn, min=-most, max=most).astype(kind)


def setup_inputs(seed: int = 0) -> dict:
    key_of = jax.random.split(jax.random.key(seed), 11)
    queries = draw_queries(jax.random.fold_in(key_of[10], 71), 0)
    keys = draw_keys(jax.random.fold_in(key_of[10], 71), 0)
    values = centred(key_of[2], (TOTAL_FRAMES, KEY_VALUE_HEADS * HEAD_SIZE), 1.0, 6.0, ((0, 512),))
    doc_ids = jnp.searchsorted(jnp.cumsum(ragged_sizes(key_of[3], 2 * N_CTX, TOTAL_FRAMES, BLOCK_FRAMES, 1)), jnp.arange(TOTAL_FRAMES), side="right").astype(jnp.int32)
    sample_rows = draw_sample_rows(jax.random.fold_in(key_of[10], 71), 0)
    owners_keys = jax.random.split(jax.random.fold_in(key_of[5], 1), SAMPLED // SAMP)
    owners_turns = jax.random.permutation(jax.random.fold_in(key_of[5], 3), SAMPLED // SAMP)
    owners = jax.vmap(lambda own, number: routed_block(jax.random.fold_in(key_of[5], 2), own, number, SAMP, N_CTX, 1, CAP, 2))(owners_keys, owners_turns).reshape((SAMPLED, 1))
    targets = place_ends(jax.random.randint(key_of[6], (SAMPLED, CB), 0, CODES), jax.random.fold_in(key_of[6], 1), 0, CODES - 1).astype(jnp.int32)
    in_proj = centred(key_of[7], (QUERY_HEADS * HEAD_SIZE, DD), (QUERY_HEADS * HEAD_SIZE) ** -0.5, 0.09375, ((0, 8),))
    dec_gain = jnp.clip(1.0 + 0.1 * jax.random.normal(key_of[8], (DD,), jnp.float32), 0.5, 1.5)
    code_heads = draw_code_heads(jax.random.fold_in(key_of[10], 71), 0)
    return {"queries": queries, "keys": keys, "values": values, "doc_ids": doc_ids, "sample_rows": sample_rows, "owners": owners, "targets": targets, "in_proj": in_proj, "dec_gain": dec_gain, "code_heads": code_heads}


def attend_block(block_index, queries, padded_keys, padded_values, doc_ids, docs_padded):
    group_width = QUERY_HEADS // KEY_VALUE_HEADS
    score_scale = 1.0 / math.sqrt(HEAD_SIZE)
    start_shift = (block_index * BLOCK_FRAMES).astype(jnp.int32)
    query_block_rows = lax.dynamic_slice_in_dim(queries, start_shift, BLOCK_FRAMES, 0).astype(jnp.float32).reshape(BLOCK_FRAMES, KEY_VALUE_HEADS, group_width, HEAD_SIZE)
    key_block_rows = lax.dynamic_slice_in_dim(padded_keys, start_shift, 2 * BLOCK_FRAMES, 0).astype(jnp.float32).reshape(2 * BLOCK_FRAMES, KEY_VALUE_HEADS, HEAD_SIZE)
    value_block_rows = lax.dynamic_slice_in_dim(padded_values, start_shift, 2 * BLOCK_FRAMES, 0).astype(jnp.float32).reshape(2 * BLOCK_FRAMES, KEY_VALUE_HEADS, HEAD_SIZE)
    query_docs = lax.dynamic_slice_in_dim(doc_ids, start_shift, BLOCK_FRAMES, 0)
    key_docs = lax.dynamic_slice_in_dim(docs_padded, start_shift, 2 * BLOCK_FRAMES, 0)
    earlier = jnp.arange(2 * BLOCK_FRAMES, dtype=jnp.int32)[None, :] - BLOCK_FRAMES <= jnp.arange(BLOCK_FRAMES, dtype=jnp.int32)[:, None]
    visible = (query_docs[:, None] == key_docs[None, :]) & earlier

    def one_head(operands):
        head_queries, head_keys, head_values = operands
        scores = jnp.einsum('qgd,kd->qgk', head_queries, head_keys) * score_scale
        scores = jnp.where(visible[:, None, :], scores, -1e+30)
        highest = lax.optimization_barrier(jnp.max(scores, axis=-1, keepdims=True))
        weights = jnp.exp(scores - highest)
        totals = lax.optimization_barrier(jnp.sum(weights, axis=-1, keepdims=True))
        rounded = lax.optimization_barrier(weights.astype(jnp.bfloat16)).astype(jnp.float32)
        mixed = jnp.einsum('qgk,kd->qgd', rounded, head_values) / totals
        return mixed.astype(jnp.bfloat16)
    per_head = lax.map(one_head, (jnp.transpose(query_block_rows, (1, 0, 2, 3)), jnp.transpose(key_block_rows, (1, 0, 2)), jnp.transpose(value_block_rows, (1, 0, 2))))
    return jnp.transpose(per_head, (1, 0, 2, 3)).reshape(BLOCK_FRAMES, QUERY_HEADS * HEAD_SIZE)

def reference(queries, keys, values, doc_ids, sample_rows, owners, targets, in_proj, dec_gain, code_heads):
    padded_keys = jnp.concatenate([jnp.zeros((BLOCK_FRAMES, KEY_VALUE_HEADS * HEAD_SIZE), keys.dtype), keys], axis=0)
    padded_values = jnp.concatenate([jnp.zeros((BLOCK_FRAMES, KEY_VALUE_HEADS * HEAD_SIZE), values.dtype), values], axis=0)
    docs_padded = jnp.concatenate([jnp.full((BLOCK_FRAMES,), -1, jnp.int32), doc_ids.astype(jnp.int32)])

    def per_block(block_index):
        return attend_block(block_index, queries, padded_keys, padded_values, doc_ids.astype(jnp.int32), docs_padded)
    attended = lax.map(per_block, jnp.arange(N_CTX, dtype=jnp.int32)).reshape(TOTAL_FRAMES, QUERY_HEADS * HEAD_SIZE)
    source = jnp.arange(SAMPLED, dtype=jnp.int32) // SAMP
    picked = jnp.take(attended, (source * BLOCK_FRAMES + sample_rows).astype(jnp.int32), axis=0)
    state = jnp.dot(picked, in_proj, preferred_element_type=jnp.float32)
    normed = (state * lax.rsqrt(lax.optimization_barrier(jnp.mean(state * state, axis=-1, keepdims=True)) + 1e-06) * dec_gain).astype(jnp.bfloat16)
    logits = jnp.einsum('sd,cdv->scv', normed.astype(jnp.float32), code_heads.astype(jnp.float32))
    row_top = lax.optimization_barrier(jnp.max(logits, axis=-1, keepdims=True))
    log_total = jnp.log(lax.optimization_barrier(jnp.sum(jnp.exp(logits - row_top), axis=-1))) + row_top[..., 0]
    target_logit = jnp.take_along_axis(logits, targets[:, :, None].astype(jnp.int32), axis=-1)[..., 0]
    frame_loss = lax.optimization_barrier(jnp.mean(log_total - target_logit, axis=-1))
    owner_ids = owners[:, 0].astype(jnp.int32)
    grouped = owner_ids.reshape(N_CTX, SAMP)
    places = jnp.arange(SAMP, dtype=jnp.int32)
    before_same = (grouped[:, None, :] == grouped[:, :, None]) & (places[None, None, :] < places[None, :, None])
    ranks = lax.optimization_barrier(jnp.sum(before_same.astype(jnp.int32), axis=-1)).reshape(SAMPLED)
    column = source * CAP + ranks
    slot_loss = jnp.zeros((N_CTX, N_CTX * CAP), jnp.float32).at[owner_ids, column].set(frame_loss)
    return (attended, slot_loss)
```

```python
import functools
import math

import jax
import jax.numpy as jnp
from jax import lax
from jax.experimental import pallas as pl
from jax.experimental.pallas import tpu as pltpu
from jax.sharding import PartitionSpec as P

HEAD_SIZE = 128
KEY_TILE = 256
MASKED = -1e30
bf16 = jnp.bfloat16
f32 = jnp.float32
VMEM = pl.BlockSpec(memory_space=pltpu.VMEM)
SMEM = pl.BlockSpec(memory_space=pltpu.SMEM)
ANY = pl.BlockSpec(memory_space=pl.ANY)


def params(mib=48):
    return pltpu.CompilerParams(vmem_limit_bytes=mib * 2**20)


def cost(flops, moved, exps=0):
    return pl.CostEstimate(flops=flops, bytes_accessed=moved, transcendentals=exps)


def shape_of(shape, dtype):
    return jax.ShapeDtypeStruct(shape, dtype)


def pack_kernel(
    group, rows_ref, keys_hbm, values_hbm, queries_hbm, out_ref, keys_ref, values_ref, queries_ref, sems
):
    heads = out_ref.shape[0]
    frames = keys_ref.shape[0]
    per_head = rows_ref.shape[0] // heads
    pieces = queries_ref.shape[0] // 32
    copies = []
    for p in range(pieces):
        rows = pl.ds(p * 32, 32)
        copies.append(
            pltpu.make_async_copy(queries_hbm.at[rows], queries_ref.at[rows], sems.at[p])
        )
    copies.append(pltpu.make_async_copy(keys_hbm, keys_ref, sems.at[pieces]))
    copies.append(pltpu.make_async_copy(values_hbm, values_ref, sems.at[pieces + 1]))
    for copy in copies:
        copy.start()
    me = lax.axis_index("head")
    row = lax.broadcasted_iota(jnp.int32, (per_head, frames), 0)
    lane = lax.broadcasted_iota(jnp.int32, (per_head, frames), 1)
    wanted = jnp.full((per_head, frames), -1, jnp.int32)
    for i in range(per_head):
        wanted = jnp.where(row == i, rows_ref[me * per_head + i] - me * frames, wanted)
    chosen = jnp.where(lane == wanted, 1.0, 0.0).astype(bf16)
    for copy in copies:
        copy.wait()
    picked = jnp.dot(chosen, queries_ref[...], preferred_element_type=f32)
    for g in range(heads):
        span = pl.ds(g * HEAD_SIZE, HEAD_SIZE)
        out_ref[g, pl.ds(0, frames), :] = keys_ref[:, span]
        out_ref[g, pl.ds(frames, frames), :] = values_ref[:, span]
        parts = [
            picked[:, (g * group + j) * HEAD_SIZE : (g * group + j + 1) * HEAD_SIZE]
            for j in range(group)
        ]
        out_ref[g, pl.ds(2 * frames, group * per_head), :] = jnp.concatenate(parts, axis=0).astype(
            bf16
        )


def block_rows(s, own_ref, first_ref, second_ref, frames, which):
    heads = own_ref.shape[0]
    half = heads // 2
    if s >= heads:
        return own_ref[s - heads, pl.ds(which * frames, frames), :]
    ref, at = (first_ref, s) if s < half else (second_ref, s - half)
    return ref[pl.ds((2 * at + which) * frames, frames), :]


def doc_rows(second_ref, docs_ref, frames):
    count = docs_ref.shape[0]
    before = second_ref[pl.ds(count * frames, 2 * count), :].astype(f32)[:count]
    return jnp.concatenate([before, docs_ref[...]], axis=0)


def unpack_kernel(
    own_ref, first_ref, second_ref, docs_ref, marks_ref, keys_ref, values_ref, all_docs_ref, low_ref
):
    heads = own_ref.shape[0]
    frames = docs_ref.shape[1]
    one = jnp.ones((frames, HEAD_SIZE), bf16)
    for s in range(2 * heads):
        rows = pl.ds(s * frames, frames)
        keys_ref[rows, :] = block_rows(s, own_ref, first_ref, second_ref, frames, 0)
        values_ref[rows, pl.ds(0, HEAD_SIZE)] = block_rows(
            s, own_ref, first_ref, second_ref, frames, 1
        )
        values_ref[rows, pl.ds(HEAD_SIZE, HEAD_SIZE)] = one
    docs = doc_rows(second_ref, docs_ref, frames)
    all_docs_ref[...] = docs
    for t in range(low_ref.shape[0]):
        below = jnp.where(docs < marks_ref[t].astype(f32), 1.0, 0.0)
        low_ref[t] = jnp.sum(below).astype(jnp.int32) // KEY_TILE


def sample_kernel(
    scale, own_ref, first_ref, second_ref, docs_ref, mine_ref, proj_ref, out_ref, scores_ref
):
    heads = own_ref.shape[0]
    frames = docs_ref.shape[1]
    extra = own_ref.shape[1] - 2 * frames
    group = proj_ref.shape[0] // HEAD_SIZE
    per_head = extra // group
    rows = heads * extra
    tile = 2 * frames
    queries = own_ref[:, pl.ds(2 * frames, extra), :].reshape(rows, HEAD_SIZE)
    docs = doc_rows(second_ref, docs_ref, frames)
    my_doc = jnp.broadcast_to(mine_ref[:, 0:1], (rows, tile))
    my_place = jnp.broadcast_to(mine_ref[:, 1:2], (rows, tile))
    lane = lax.broadcasted_iota(jnp.int32, (rows, tile), 1).astype(f32)
    highest = jnp.full((rows, HEAD_SIZE), MASKED, f32)
    for s in range(0, 2 * heads, 2):
        key_tile = jnp.concatenate(
            [block_rows(s + i, own_ref, first_ref, second_ref, frames, 0) for i in range(2)], axis=0
        )
        scores = lax.dot_general(
            queries, key_tile, (((1,), (1,)), ((), ())), preferred_element_type=f32
        )
        tile_docs = jnp.concatenate([docs[s : s + 1], docs[s + 1 : s + 2]], axis=1)
        seen = (tile_docs == my_doc) & (lane <= my_place - s * frames)
        scores = jnp.where(seen, scores * scale, MASKED)
        start = s * frames
        scores_ref[:, start : start + tile] = scores
        for part in range(tile // HEAD_SIZE):
            highest = jnp.maximum(highest, scores[:, part * HEAD_SIZE : (part + 1) * HEAD_SIZE])
    top = jnp.max(highest, axis=1, keepdims=True)
    total = jnp.zeros((rows, HEAD_SIZE), f32)
    mixed = jnp.zeros((rows, HEAD_SIZE), f32)
    for s in range(0, 2 * heads, 2):
        value_tile = jnp.concatenate(
            [block_rows(s + i, own_ref, first_ref, second_ref, frames, 1) for i in range(2)], axis=0
        )
        start = s * frames
        weights = jnp.exp2(scores_ref[:, start : start + tile] - top)
        for part in range(tile // HEAD_SIZE):
            total = total + weights[:, part * HEAD_SIZE : (part + 1) * HEAD_SIZE]
        mixed = mixed + jnp.dot(weights.astype(bf16), value_tile, preferred_element_type=f32)
    attended = mixed / jnp.sum(total, axis=1, keepdims=True)
    by_group = attended.reshape(heads, group, per_head, HEAD_SIZE)
    state = jnp.zeros((heads * per_head, proj_ref.shape[1]), f32)
    for j in range(group):
        part = by_group[:, j].reshape(heads * per_head, HEAD_SIZE).astype(bf16)
        state = state + jnp.dot(
            part, proj_ref[pl.ds(j * HEAD_SIZE, HEAD_SIZE), :], preferred_element_type=f32
        )
    state = state.astype(bf16)
    for d in range(heads):
        out_ref[d] = state


def logits_kernel(parts_ref, gain_ref, codes_ref, targets_ref, out_ref):
    heads, samples, width = parts_ref.shape
    books, _, codes = codes_ref.shape
    state = parts_ref[0].astype(f32)
    for s in range(1, heads):
        state = state + parts_ref[s].astype(f32)
    square = jnp.sum(state * state, axis=1, keepdims=True)
    normed = (state * lax.rsqrt(square / width + 1e-06) * gain_ref[...]).astype(bf16)
    lane = lax.broadcasted_iota(jnp.int32, (samples, 128), 1)
    code = lax.broadcasted_iota(jnp.int32, (samples, codes), 1)
    stats = jnp.zeros((samples, 128), f32)
    for b in range(books):
        logits = jnp.dot(normed, codes_ref[b], preferred_element_type=f32)
        top = jnp.max(logits, axis=1, keepdims=True)
        mass = jnp.sum(jnp.exp(logits - top), axis=1, keepdims=True)
        hit = code == targets_ref[:, b : b + 1]
        target = jnp.sum(jnp.where(hit, logits, 0.0), axis=1, keepdims=True)
        for k, column in enumerate((top, mass, target)):
            stats = jnp.where(lane == 3 * b + k, column, stats)
    padded = jnp.concatenate([stats, jnp.zeros((128 - samples, 128), f32)], axis=0)
    across = jnp.transpose(padded)[:8]
    for d in range(heads):
        out_ref[d] = across


def place_kernel(books, stats_ref, owner_ref, column_ref, out_ref):
    heads = stats_ref.shape[0]
    loss = jnp.zeros((1, 128), f32)
    for b in range(books):
        tops = [stats_ref[s, 3 * b : 3 * b + 1, :] for s in range(heads)]
        top = functools.reduce(jnp.maximum, tops)
        mass = jnp.zeros((1, 128), f32)
        target = jnp.zeros((1, 128), f32)
        for s in range(heads):
            mass = mass + stats_ref[s, 3 * b + 1 : 3 * b + 2, :] * jnp.exp(tops[s] - top)
            target = target + stats_ref[s, 3 * b + 2 : 3 * b + 3, :]
        loss = loss + (jnp.log(mass) + top - target)
    loss = loss * (1.0 / books)
    spread = jnp.where(owner_ref[...] > 0.0, loss, 0.0)
    out_ref[...] = jnp.dot(
        spread, column_ref[...], preferred_element_type=f32, precision=lax.Precision.HIGHEST
    )


def main_kernel(scale, first_tile, low_ref, queries_ref, keys_ref, values_ref, docs_ref, across_ref, *refs):
    out_ref, bias_ref, scores_ref = refs[-3:]
    tile, width = queries_ref.shape
    group = width // HEAD_SIZE
    block = keys_ref.shape[0] // 2
    number = first_tile + pl.program_id(0)
    start = block + number * tile
    low = low_ref[number]
    high = (start + tile + KEY_TILE - 1) // KEY_TILE
    halves = KEY_TILE // HEAD_SIZE

    def body(count):
        base = pl.multiple_of(low * KEY_TILE, KEY_TILE)
        my_doc = jnp.broadcast_to(docs_ref[...], (tile, HEAD_SIZE))
        ahead = lax.broadcasted_iota(jnp.int32, (tile, HEAD_SIZE), 0) - lax.broadcasted_iota(
            jnp.int32, (tile, HEAD_SIZE), 1
        )
        for k in range(count * halves):
            doc = across_ref[pl.ds(low * halves + k, 1), :]
            seen = (doc == my_doc) & (ahead >= base + k * HEAD_SIZE - start)
            bias_ref[:, k * HEAD_SIZE : (k + 1) * HEAD_SIZE] = jnp.where(seen, 0.0, MASKED)
        for j in range(group):
            queries = queries_ref[:, j * HEAD_SIZE : (j + 1) * HEAD_SIZE]
            highest = jnp.full((tile, HEAD_SIZE), MASKED, f32)
            for k in range(count):
                span = slice(k * KEY_TILE, (k + 1) * KEY_TILE)
                key_tile = keys_ref[pl.ds(base + k * KEY_TILE, KEY_TILE), :]
                scores = lax.dot_general(
                    queries, key_tile, (((1,), (1,)), ((), ())), preferred_element_type=f32
                )
                scores = scores * scale + bias_ref[:, span]
                scores_ref[j, :, span] = scores
                highest = jnp.maximum(
                    highest, jnp.maximum(scores[:, :HEAD_SIZE], scores[:, HEAD_SIZE:])
                )
            top = jnp.max(highest, axis=1, keepdims=True)
            mixed = None
            for k in range(count):
                span = slice(k * KEY_TILE, (k + 1) * KEY_TILE)
                weights = jnp.exp2(scores_ref[j, :, span] - top).astype(bf16)
                value_tile = values_ref[pl.ds(base + k * KEY_TILE, KEY_TILE), :]
                part = jnp.dot(weights, value_tile, preferred_element_type=f32)
                mixed = part if mixed is None else mixed + part
            out_ref[:, j * HEAD_SIZE : (j + 1) * HEAD_SIZE] = (
                mixed[:, :HEAD_SIZE] / mixed[:, HEAD_SIZE:]
            ).astype(bf16)

    most = scores_ref.shape[2] // KEY_TILE
    for count in range(1, most + 1):
        pl.when(high - low == count)(functools.partial(body, count))


def attend(scale, first_tile, tiles, low, queries, keys, values, docs, across, before):
    block, width = queries.shape
    tile = HEAD_SIZE
    group = width // HEAD_SIZE
    most = (block + tile + KEY_TILE - 1) // KEY_TILE
    rows = lambda i: (first_tile + i, 0)
    whole = lambda i: (0, 0)
    in_specs = [
        SMEM,
        pl.BlockSpec((tile, width), rows),
        pl.BlockSpec(keys.shape, whole),
        pl.BlockSpec(values.shape, whole),
        pl.BlockSpec((tile, 1), rows),
        pl.BlockSpec(across.shape, whole),
    ]
    operands = [low, queries, keys, values, docs, across]
    aliases = {}
    if before is not None:
        in_specs.append(pl.BlockSpec(memory_space=pl.ANY))
        operands.append(before)
        aliases = {len(operands) - 1: 0}
    pairs = tiles * group * tile * 4 * KEY_TILE
    return pl.pallas_call(
        functools.partial(main_kernel, scale, first_tile),
        grid=(tiles,),
        out_shape=shape_of((block, width), bf16),
        in_specs=in_specs,
        out_specs=pl.BlockSpec((tile, width), rows),
        scratch_shapes=[
            pltpu.VMEM((tile, most * KEY_TILE), f32),
            pltpu.VMEM((group, tile, most * KEY_TILE), f32),
        ],
        input_output_aliases=aliases,
        compiler_params=params(),
        cost_estimate=cost(pairs * 6 * HEAD_SIZE, 2 * 2**20, pairs),
    )(*operands)


def to_heads(value):
    return lax.all_to_all(value, "head", split_axis=0, concat_axis=0, tiled=True)


def after(value, *others):
    return lax.optimization_barrier((value, *others))[0]


def local(
    queries, keys, values, doc_ids, sample_rows, owners, targets, in_proj, dec_gain, code_heads
):
    heads = lax.axis_size("head")
    contexts = lax.axis_size("ctx")
    head_number = lax.axis_index("head")
    ctx_number = lax.axis_index("ctx")
    frames = keys.shape[0]
    block = doc_ids.shape[0]
    samples = sample_rows.shape[0]
    per_head = samples // heads
    width = queries.shape[1] // heads
    group = width // HEAD_SIZE
    scale = math.log2(math.e) / math.sqrt(HEAD_SIZE)
    deep = in_proj.shape[1]
    books = targets.shape[1]

    packed = pl.pallas_call(
        functools.partial(pack_kernel, group),
        out_shape=shape_of((heads, 2 * frames + group * per_head, HEAD_SIZE), bf16),
        in_specs=[SMEM, ANY, ANY, ANY],
        out_specs=VMEM,
        scratch_shapes=[
            pltpu.VMEM(keys.shape, bf16),
            pltpu.VMEM(values.shape, bf16),
            pltpu.VMEM(queries.shape, bf16),
            pltpu.SemaphoreType.DMA((frames // 32 + 2,)),
        ],
        compiler_params=params(56),
        cost_estimate=cost(2 * per_head * frames * queries.shape[1], 2 * 2**20),
    )(sample_rows, keys, values, queries)
    own = to_heads(packed)

    ring = [(s, (s + 1) % contexts) for s in range(contexts)]
    half = heads // 2
    marked = doc_ids + 1
    told = jnp.where(ctx_number == contexts - 1, 0, marked).astype(bf16).reshape(heads, frames)
    first = own[:half, : 2 * frames].reshape(block, HEAD_SIZE)
    second = own[half:, : 2 * frames].reshape(block, HEAD_SIZE)
    second = jnp.concatenate([second, told, jnp.zeros_like(told)], axis=0)
    first = lax.ppermute(first, "ctx", ring)
    second = lax.ppermute(second, "ctx", ring)
    by_head = jnp.transpose(queries.reshape(frames, heads, width), (1, 0, 2))
    queries_here = to_heads(after(by_head, own)).reshape(block, width)

    docs = marked.astype(f32).reshape(heads, frames)
    spots = jnp.arange(block, dtype=jnp.int32)
    sample_docs = jnp.sum(
        jnp.where(sample_rows[:, None] == spots[None, :], marked[None, :], 0), axis=1
    )
    mine = jnp.stack([sample_docs, sample_rows + block], axis=1).astype(f32)
    mine = jnp.broadcast_to(
        mine.reshape(heads, 1, per_head, 2), (heads, group, per_head, 2)
    ).reshape(heads * group * per_head, 2)

    shares = pl.pallas_call(
        functools.partial(sample_kernel, scale),
        out_shape=shape_of((heads, samples, deep), bf16),
        in_specs=[VMEM] * 6,
        out_specs=VMEM,
        scratch_shapes=[pltpu.VMEM((samples * group, 2 * block), f32)],
        compiler_params=params(),
        cost_estimate=cost(
            4 * samples * group * 2 * block * HEAD_SIZE, 4 * 2**20, samples * group * 2 * block
        ),
    )(own, first, second, docs, mine, in_proj)

    all_keys, all_values, across, low = pl.pallas_call(
        unpack_kernel,
        out_shape=(
            shape_of((2 * block, HEAD_SIZE), bf16),
            shape_of((2 * block, 2 * HEAD_SIZE), bf16),
            shape_of((2 * heads, frames), f32),
            shape_of((block // HEAD_SIZE,), jnp.int32),
        ),
        in_specs=[VMEM] * 4 + [SMEM],
        out_specs=(VMEM, VMEM, VMEM, SMEM),
        compiler_params=params(),
        cost_estimate=cost(0, 3 * 2**20),
    )(after(own, shares), first, second, docs, marked[::HEAD_SIZE])

    parts = to_heads(after(shares, queries_here))
    tiles = block // HEAD_SIZE
    attended = attend(
        scale,
        0,
        tiles,
        low,
        queries_here,
        all_keys,
        all_values,
        marked.astype(f32)[:, None],
        across,
        None,
    )
    parts, attended = lax.optimization_barrier((parts, attended))

    codes_here = code_heads.shape[2]
    stats = pl.pallas_call(
        logits_kernel,
        out_shape=shape_of((heads, 8, 128), f32),
        in_specs=[VMEM] * 4,
        out_specs=VMEM,
        compiler_params=params(),
        cost_estimate=cost(4 * samples * deep * codes_here * books, code_heads.size * 2),
    )(parts, dec_gain[None, :], code_heads, targets - head_number * codes_here)
    all_stats = to_heads(stats)

    owner_ids = owners[:, 0]
    positions = jnp.arange(samples, dtype=jnp.int32)
    same = (owner_ids[None, :] == owner_ids[:, None]) & (positions[None, :] < positions[:, None])
    ranks = jnp.sum(same.astype(jnp.int32), axis=1)
    owner_pad = jnp.concatenate([owner_ids, jnp.full((128 - samples,), -1, jnp.int32)])
    slot_count = 2 * contexts
    owner_hit = (owner_pad[None, :] == jnp.arange(contexts)[:, None]).astype(f32)
    slots = jnp.concatenate([2 * ctx_number + ranks, jnp.full((128 - samples,), -1, jnp.int32)])
    slot_hit = (slots[:, None] == jnp.arange(slot_count)[None, :]).astype(f32)
    placed = pl.pallas_call(
        functools.partial(place_kernel, books),
        out_shape=shape_of((contexts, slot_count), f32),
        in_specs=[VMEM] * 3,
        out_specs=VMEM,
        compiler_params=params(),
        cost_estimate=cost(10**6, 10**5),
    )(all_stats, owner_hit, slot_hit)
    arrived = lax.all_to_all(placed, "ctx", split_axis=0, concat_axis=0, tiled=True)
    slot_loss = jnp.sum(arrived, axis=0, keepdims=True)
    return (attended, slot_loss)


def solution(mesh):
    in_specs = (
        P(("ctx", "head"), None),
        P(("ctx", "head"), None),
        P(("ctx", "head"), None),
        P("ctx"),
        P("ctx"),
        P("ctx", None),
        P("ctx", None),
        P("head", None),
        P(),
        P(None, None, "head"),
    )
    out_specs = (P("ctx", "head"), P("ctx", None))
    return jax.shard_map(local, mesh=mesh, in_specs=in_specs, out_specs=out_specs, check_vma=False)
```

```python
import functools
import math

import jax
import jax.numpy as jnp
from jax import lax
from jax.experimental import pallas as pl
from jax.experimental.pallas import tpu as pltpu
from jax.sharding import PartitionSpec as P

HEAD_SIZE = 128
KEY_TILE = 256
CUT = 4
QUERY_TILE = 256
MASKED = -1e30
bf16 = jnp.bfloat16
f32 = jnp.float32
VMEM = pl.BlockSpec(memory_space=pltpu.VMEM)
SMEM = pl.BlockSpec(memory_space=pltpu.SMEM)
ANY = pl.BlockSpec(memory_space=pl.ANY)


def params(mib=14):
    return pltpu.CompilerParams(vmem_limit_bytes=mib * 2**20)


def cost(flops, moved, exps=0):
    return pl.CostEstimate(flops=flops, bytes_accessed=moved, transcendentals=exps)


def shape_of(shape, dtype):
    return jax.ShapeDtypeStruct(shape, dtype)


def pack_kernel(group, rows_ref, keys_hbm, values_hbm, queries_hbm, out_ref, queries_ref, sems):
    heads = out_ref.shape[0]
    frames = queries_ref.shape[0]
    per_head = rows_ref.shape[0] // heads
    copies = []
    for which, ref in enumerate((keys_hbm, values_hbm)):
        for g in range(heads):
            copies.append(
                pltpu.make_async_copy(
                    ref.at[:, pl.ds(g * HEAD_SIZE, HEAD_SIZE)],
                    out_ref.at[g, pl.ds(which * frames, frames), :],
                    sems.at[which * heads + g],
                )
            )
    pieces = []
    for p in range(4):
        span = pl.ds(p * (frames // 4), frames // 4)
        pieces.append(
            pltpu.make_async_copy(
                queries_hbm.at[span], queries_ref.at[span], sems.at[2 * heads + p]
            )
        )
    for copy in pieces + copies:
        copy.start()
    me = lax.axis_index("head")
    row = lax.broadcasted_iota(jnp.int32, (per_head, frames), 0)
    lane = lax.broadcasted_iota(jnp.int32, (per_head, frames), 1)
    wanted = jnp.full((per_head, frames), -1, jnp.int32)
    for i in range(per_head):
        wanted = jnp.where(row == i, rows_ref[me * per_head + i] - me * frames, wanted)
    chosen = jnp.where(lane == wanted, 1.0, 0.0).astype(bf16)
    for copy in pieces:
        copy.wait()
    picked = jnp.dot(chosen, queries_ref[...], preferred_element_type=f32)
    for g in range(heads):
        parts = [
            picked[:, (g * group + j) * HEAD_SIZE : (g * group + j + 1) * HEAD_SIZE]
            for j in range(group)
        ]
        out_ref[g, pl.ds(2 * frames, group * per_head), :] = jnp.concatenate(parts, axis=0).astype(
            bf16
        )
    for copy in copies:
        copy.wait()


def turned(row):
    return jnp.transpose(jnp.broadcast_to(row, (128, 128)))


def prep_kernel(
    group, rows_ref, ids_ref, owners_ref, targets_ref, docs_ref, told_ref, mine_ref, info_ref
):
    heads, frames = ids_ref.shape
    samples = rows_ref.shape[0]
    per_head = samples // heads
    docs = (ids_ref[...] + 1).astype(f32)
    docs_ref[...] = docs
    last = lax.axis_index("ctx") == lax.axis_size("ctx") - 1
    told_ref[...] = jnp.where(last, 0.0, docs)
    row = lax.broadcasted_iota(jnp.int32, (per_head, frames), 0)
    lane = lax.broadcasted_iota(jnp.int32, (per_head, frames), 1)
    for s in range(heads):
        place = jnp.zeros((per_head, frames), jnp.int32)
        for i in range(per_head):
            place = jnp.where(row == i, rows_ref[s * per_head + i] - s * frames, place)
        doc = jnp.sum(jnp.where(lane == place, docs[s : s + 1], 0.0), axis=1, keepdims=True)
        spot = ((heads + s) * frames + place).astype(f32)
        both = jnp.where(lane == 0, doc, spot)
        for j in range(group):
            mine_ref[pl.ds((s * group + j) * per_head, per_head), :] = both
    info_ref[...] = jnp.full(info_ref.shape, -1.0, f32)
    info_ref[0:1, 0:samples] = owners_ref[...].astype(f32)
    info_ref[2 : 2 + targets_ref.shape[0], 0:samples] = targets_ref[...].astype(f32)
    across = jnp.broadcast_to(info_ref[0:1, :], (128, 128))
    row = lax.broadcasted_iota(jnp.int32, (128, 128), 0)
    lane = lax.broadcasted_iota(jnp.int32, (128, 128), 1)
    same = (jnp.transpose(across) == across) & (row < lane)
    rank = jnp.sum(jnp.where(same, 1.0, 0.0), axis=0, keepdims=True)
    info_ref[1:2, :] = rank + (2 * lax.axis_index("ctx")).astype(f32)


def block_rows(s, own_ref, first_ref, second_ref, frames, which):
    heads = own_ref.shape[0]
    half = heads // 2
    if s >= heads:
        return own_ref[s - heads, pl.ds(which * frames, frames), :]
    ref, at = (first_ref, s) if s < half else (second_ref, s - half)
    return ref[pl.ds((2 * at + which) * frames, frames), :]


def unpack_kernel(
    own_ref, first_ref, second_ref, before_ref, docs_ref, keys_ref, values_ref, all_docs_ref, low_ref
):
    heads = own_ref.shape[0]
    frames = docs_ref.shape[1]
    for s in range(2 * heads):
        rows = pl.ds(s * frames, frames)
        keys_ref[rows, :] = block_rows(s, own_ref, first_ref, second_ref, frames, 0)
        values_ref[rows, :] = block_rows(s, own_ref, first_ref, second_ref, frames, 1)
    docs = jnp.concatenate([before_ref[...], docs_ref[...]], axis=0)
    all_docs_ref[...] = docs
    for t in range(low_ref.shape[0]):
        below = jnp.where(docs < docs_ref[t : t + 1, 0:1], 1.0, 0.0)
        low_ref[t] = jnp.sum(below).astype(jnp.int32) // KEY_TILE


def sample_kernel(
    scale,
    own_ref,
    first_ref,
    second_ref,
    before_ref,
    docs_ref,
    mine_ref,
    proj_ref,
    keep_ref,
    send_ref,
    scores_ref,
):
    heads = own_ref.shape[0]
    frames = docs_ref.shape[1]
    extra = own_ref.shape[1] - 2 * frames
    group = proj_ref.shape[0] // HEAD_SIZE
    per_head = extra // group
    rows = heads * extra
    tile = 2 * frames
    queries = own_ref[:, pl.ds(2 * frames, extra), :].reshape(rows, HEAD_SIZE)
    docs = jnp.concatenate([before_ref[...], docs_ref[...]], axis=0)
    my_doc = jnp.broadcast_to(mine_ref[:, 0:1], (rows, tile))
    my_place = jnp.broadcast_to(mine_ref[:, 1:2], (rows, tile))
    lane = lax.broadcasted_iota(jnp.int32, (rows, tile), 1).astype(f32)
    highest = jnp.full((rows, HEAD_SIZE), MASKED, f32)
    for s in range(0, 2 * heads, 2):
        key_tile = jnp.concatenate(
            [block_rows(s + i, own_ref, first_ref, second_ref, frames, 0) for i in range(2)], axis=0
        )
        scores = lax.dot_general(
            queries, key_tile, (((1,), (1,)), ((), ())), preferred_element_type=f32
        )
        tile_docs = jnp.concatenate([docs[s : s + 1], docs[s + 1 : s + 2]], axis=1)
        seen = (tile_docs == my_doc) & (lane <= my_place - s * frames)
        scores = jnp.where(seen, scores * scale, MASKED)
        start = s * frames
        scores_ref[:, start : start + tile] = scores
        for part in range(tile // HEAD_SIZE):
            highest = jnp.maximum(highest, scores[:, part * HEAD_SIZE : (part + 1) * HEAD_SIZE])
    top = jnp.max(highest, axis=1, keepdims=True)
    total = jnp.zeros((rows, HEAD_SIZE), f32)
    mixed = jnp.zeros((rows, HEAD_SIZE), f32)
    for s in range(0, 2 * heads, 2):
        value_tile = jnp.concatenate(
            [block_rows(s + i, own_ref, first_ref, second_ref, frames, 1) for i in range(2)], axis=0
        )
        start = s * frames
        weights = jnp.exp2(scores_ref[:, start : start + tile] - top)
        for part in range(tile // HEAD_SIZE):
            total = total + weights[:, part * HEAD_SIZE : (part + 1) * HEAD_SIZE]
        mixed = mixed + jnp.dot(weights.astype(bf16), value_tile, preferred_element_type=f32)
    attended = mixed / jnp.sum(total, axis=1, keepdims=True)
    by_group = attended.reshape(heads, group, per_head, HEAD_SIZE)
    state = jnp.zeros((heads * per_head, proj_ref.shape[1]), f32)
    for j in range(group):
        part = by_group[:, j].reshape(heads * per_head, HEAD_SIZE).astype(bf16)
        state = state + jnp.dot(
            part, proj_ref[pl.ds(j * HEAD_SIZE, HEAD_SIZE), :], preferred_element_type=f32
        )
    rows = state.shape[0] // 2
    odd = lax.rem(lax.axis_index("head"), 2) == 1
    keep_ref[...] = jnp.where(odd, state[rows:], state[:rows])
    send_ref[...] = jnp.where(odd, state[:rows], state[rows:]).astype(bf16)


def pair_kernel(keep_ref, came_ref, out_ref):
    state = (keep_ref[...] + came_ref[...].astype(f32)).astype(bf16)
    for d in range(out_ref.shape[0]):
        out_ref[d] = state


def logits_kernel(parts_ref, gain_ref, codes_ref, other_ref, info_ref, out_ref):
    count, samples, width = parts_ref.shape
    books, _, codes = codes_ref.shape
    me = lax.axis_index("head")
    odd = lax.rem(me, 2) == 1
    other = jnp.where(odd, me - 1, me + 1)
    state = parts_ref[0].astype(f32)
    for s in range(1, count):
        state = state + parts_ref[s].astype(f32)
    square = jnp.sum(state * state, axis=1, keepdims=True)
    normed = (state * lax.rsqrt(square / width + 1e-06) * gain_ref[...]).astype(bf16)
    lane = lax.broadcasted_iota(jnp.int32, (samples, 128), 1)
    code = lax.broadcasted_iota(jnp.int32, (samples, codes), 1).astype(f32)
    stats = jnp.zeros((samples, 128), f32)
    for b in range(books):
        first = jnp.dot(normed, codes_ref[b], preferred_element_type=f32)
        second = jnp.dot(normed, other_ref[b], preferred_element_type=f32)
        top = jnp.max(jnp.maximum(first, second), axis=1, keepdims=True)
        mass = jnp.sum(jnp.exp(first - top) + jnp.exp(second - top), axis=1, keepdims=True)
        column = turned(info_ref[2 + b : 3 + b, :])
        wanted = jnp.where(odd, column[samples : 2 * samples], column[:samples])[:, 0:1]
        hit = jnp.where(code == wanted - (me * codes).astype(f32), first, 0.0)
        hit = hit + jnp.where(code == wanted - (other * codes).astype(f32), second, 0.0)
        target = jnp.sum(hit, axis=1, keepdims=True)
        for k, figure in enumerate((top, mass, target)):
            stats = jnp.where(lane == 3 * b + k, figure, stats)
    none = jnp.zeros((samples, 128), f32)
    padded = jnp.concatenate(
        [jnp.where(odd, none, stats), jnp.where(odd, stats, none), none, none], axis=0
    )
    across = jnp.transpose(padded)[:8]
    for d in range(out_ref.shape[0]):
        out_ref[d] = across


def place_kernel(books, samples, stats_ref, info_ref, out_ref):
    heads = stats_ref.shape[0]
    losses = []
    for core in range(2):
        loss = jnp.zeros((1, 128), f32)
        for b in range(books):
            tops = [stats_ref[s, 3 * b : 3 * b + 1, :] for s in range(core, heads, 2)]
            top = functools.reduce(jnp.maximum, tops)
            mass = jnp.zeros((1, 128), f32)
            target = jnp.zeros((1, 128), f32)
            for i, s in enumerate(range(core, heads, 2)):
                mass = mass + stats_ref[s, 3 * b + 1 : 3 * b + 2, :] * jnp.exp(tops[i] - top)
                target = target + stats_ref[s, 3 * b + 2 : 3 * b + 3, :]
            loss = loss + (jnp.log(mass) + top - target)
        losses.append(loss * (1.0 / books))
    lane = lax.broadcasted_iota(jnp.int32, (1, 128), 1)
    loss = jnp.where(lane < samples // 2, losses[0], losses[1])
    contexts, slots = out_ref.shape
    owner = lax.broadcasted_iota(jnp.int32, (contexts, 128), 0).astype(f32)
    spread = jnp.where(info_ref[0:1, :] == owner, loss, 0.0)
    column = lax.broadcasted_iota(jnp.int32, (128, 128), 1).astype(f32)
    column = jnp.where(turned(info_ref[1:2, :]) == column, 1.0, 0.0)[:, :slots]
    out_ref[...] = jnp.dot(
        spread, column, preferred_element_type=f32, precision=lax.Precision.HIGHEST
    )


def main_kernel(scale, first_tile, low_ref, queries_ref, keys_ref, values_ref, across_ref, *refs):
    out_ref, bias_ref, scores_ref = refs[-3:]
    tile, width = queries_ref.shape
    group = width // HEAD_SIZE
    parts = tile // HEAD_SIZE
    block = keys_ref.shape[0] // 2
    number = first_tile + pl.program_id(0)
    start = block + number * tile
    low = low_ref[number * parts]
    high = (start + tile + KEY_TILE - 1) // KEY_TILE
    halves = KEY_TILE // HEAD_SIZE
    units = [(j, r) for j in range(group) for r in range(parts)]

    def body(count):
        base = pl.multiple_of(low * KEY_TILE, KEY_TILE)
        ahead = lax.broadcasted_iota(jnp.int32, (HEAD_SIZE, HEAD_SIZE), 0) - lax.broadcasted_iota(
            jnp.int32, (HEAD_SIZE, HEAD_SIZE), 1
        )
        for r in range(parts):
            row = (block + number * tile) // HEAD_SIZE + r
            my_doc = turned(across_ref[pl.ds(row, 1), :])
            for k in range(count * halves):
                doc = across_ref[pl.ds(low * halves + k, 1), :]
                seen = (doc == my_doc) & (ahead >= base + k * HEAD_SIZE - start - r * HEAD_SIZE)
                bias_ref[r, :, k * HEAD_SIZE : (k + 1) * HEAD_SIZE] = jnp.where(seen, 0.0, MASKED)
        tops = []
        for u, (j, r) in enumerate(units):
            queries = queries_ref[r * HEAD_SIZE : (r + 1) * HEAD_SIZE, j * HEAD_SIZE : (j + 1) * HEAD_SIZE]
            highest = None
            for k in range(count):
                span = slice(k * KEY_TILE, (k + 1) * KEY_TILE)
                key_tile = keys_ref[pl.ds(base + k * KEY_TILE, KEY_TILE), :]
                scores = lax.dot_general(
                    queries, key_tile, (((1,), (1,)), ((), ())), preferred_element_type=f32
                )
                scores = scores * scale + bias_ref[r, :, span]
                scores_ref[u, :, span] = scores
                most = jnp.maximum(scores[:, :HEAD_SIZE], scores[:, HEAD_SIZE:])
                highest = most if highest is None else jnp.maximum(highest, most)
            tops.append(jnp.max(highest, axis=1, keepdims=True))
        one = jnp.ones((count * KEY_TILE, HEAD_SIZE), bf16)
        value_rows = jnp.concatenate([values_ref[pl.ds(base, count * KEY_TILE), :], one], axis=1)
        for u, (j, r) in enumerate(units):
            weights = jnp.concatenate(
                [
                    jnp.exp2(scores_ref[u, :, k * KEY_TILE : (k + 1) * KEY_TILE] - tops[u]).astype(bf16)
                    for k in range(count)
                ],
                axis=1,
            )
            mixed = jnp.dot(weights, value_rows, preferred_element_type=f32)
            out_ref[r * HEAD_SIZE : (r + 1) * HEAD_SIZE, j * HEAD_SIZE : (j + 1) * HEAD_SIZE] = (
                mixed[:, :HEAD_SIZE] / mixed[:, HEAD_SIZE:]
            ).astype(bf16)

    most = scores_ref.shape[2] // KEY_TILE
    for count in range(1, most + 1):
        pl.when(high - low == count)(functools.partial(body, count))


def attend(scale, first_tile, tiles, low, queries, keys, values, across, before):
    block, width = queries.shape
    tile = QUERY_TILE
    first_tile, tiles = first_tile * HEAD_SIZE // tile, tiles * HEAD_SIZE // tile
    group = width // HEAD_SIZE
    most = (block + tile + KEY_TILE - 1) // KEY_TILE
    rows = lambda i: (first_tile + i, 0)
    whole = lambda i: (0, 0)
    in_specs = [
        SMEM,
        pl.BlockSpec((tile, width), rows),
        pl.BlockSpec(keys.shape, whole),
        pl.BlockSpec(values.shape, whole),
        pl.BlockSpec(across.shape, whole),
    ]
    operands = [low, queries, keys, values, across]
    aliases = {}
    if before is not None:
        in_specs.append(pl.BlockSpec(memory_space=pl.ANY))
        operands.append(before)
        aliases = {len(operands) - 1: 0}
    pairs = tiles * group * tile * 4 * KEY_TILE
    return pl.pallas_call(
        functools.partial(main_kernel, scale, first_tile),
        grid=(tiles,),
        out_shape=shape_of((block, width), bf16),
        in_specs=in_specs,
        out_specs=pl.BlockSpec((tile, width), rows),
        scratch_shapes=[
            pltpu.VMEM((tile // HEAD_SIZE, HEAD_SIZE, most * KEY_TILE), f32),
            pltpu.VMEM((group * tile // HEAD_SIZE, HEAD_SIZE, most * KEY_TILE), f32),
        ],
        input_output_aliases=aliases,
        compiler_params=params(),
        cost_estimate=cost(pairs * 6 * HEAD_SIZE, 2 * 2**20, pairs),
    )(*operands)


def to_heads(value):
    return lax.all_to_all(value, "head", split_axis=0, concat_axis=0, tiled=True)


def after(value, *others):
    return lax.optimization_barrier((value, *others))[0]


def local(
    queries, keys, values, doc_ids, sample_rows, owners, targets, in_proj, dec_gain, code_heads
):
    heads = lax.axis_size("head")
    contexts = lax.axis_size("ctx")
    head_number = lax.axis_index("head")
    ctx_number = lax.axis_index("ctx")
    frames = keys.shape[0]
    block = doc_ids.shape[0]
    samples = sample_rows.shape[0]
    per_head = samples // heads
    width = queries.shape[1] // heads
    group = width // HEAD_SIZE
    scale = math.log2(math.e) / math.sqrt(HEAD_SIZE)
    deep = in_proj.shape[1]
    books = targets.shape[1]

    packed = pl.pallas_call(
        functools.partial(pack_kernel, group),
        out_shape=shape_of((heads, 2 * frames + group * per_head, HEAD_SIZE), bf16),
        in_specs=[SMEM, ANY, ANY, ANY],
        out_specs=VMEM,
        scratch_shapes=[
            pltpu.VMEM(queries.shape, bf16),
            pltpu.SemaphoreType.DMA((2 * heads + 4,)),
        ],
        compiler_params=params(56),
        cost_estimate=cost(2 * per_head * frames * queries.shape[1], 2 * 2**20),
    )(sample_rows, keys, values, queries)
    own = to_heads(packed)

    docs, told, mine, info = pl.pallas_call(
        functools.partial(prep_kernel, group),
        out_shape=(
            shape_of((heads, frames), f32),
            shape_of((heads, frames), f32),
            shape_of((samples * group, 128), f32),
            shape_of((8, 128), f32),
        ),
        in_specs=[SMEM, VMEM, VMEM, VMEM],
        out_specs=(VMEM,) * 4,
        compiler_params=params(8),
        cost_estimate=cost(10**6, 4 * 10**5),
    )(
        after(sample_rows, packed),
        doc_ids.reshape(heads, frames),
        owners.reshape(1, samples),
        targets.T,
    )
    ring = [(s, (s + 1) % contexts) for s in range(contexts)]
    half = heads // 2
    before = lax.ppermute(told, "ctx", ring)
    by_head = jnp.transpose(after(queries, packed).reshape(frames, heads, width), (1, 0, 2))
    own, docs, mine, before, by_head = lax.optimization_barrier((own, docs, mine, before, by_head))
    first = own[:half, : 2 * frames].reshape(block, HEAD_SIZE)
    second = own[half:, : 2 * frames].reshape(block, HEAD_SIZE)
    first = lax.ppermute(first, "ctx", ring)
    second = lax.ppermute(second, "ctx", ring)
    queries_here = to_heads(by_head).reshape(block, width)
    pairs = [(s, s + 1 - 2 * (s % 2)) for s in range(heads)]
    other_codes = lax.ppermute(after(code_heads, own), "head", pairs)

    keep, send = pl.pallas_call(
        functools.partial(sample_kernel, scale),
        out_shape=(shape_of((samples // 2, deep), f32), shape_of((samples // 2, deep), bf16)),
        in_specs=[VMEM] * 7,
        out_specs=(VMEM, VMEM),
        scratch_shapes=[pltpu.VMEM((samples * group, 2 * block), f32)],
        compiler_params=params(),
        cost_estimate=cost(
            240 * samples * group * 2 * block * HEAD_SIZE, 4 * 2**20, samples * group * 2 * block
        ),
    )(own, first, second, before, docs, mine, in_proj)
    came = lax.ppermute(send, "head", pairs)

    all_keys, all_values, across, low = pl.pallas_call(
        unpack_kernel,
        out_shape=(
            shape_of((2 * block, HEAD_SIZE), bf16),
            shape_of((2 * block, HEAD_SIZE), bf16),
            shape_of((2 * heads, frames), f32),
            shape_of((block // HEAD_SIZE,), jnp.int32),
        ),
        in_specs=[VMEM] * 5,
        out_specs=(VMEM, VMEM, VMEM, SMEM),
        compiler_params=params(),
        cost_estimate=cost(0, 2 * 2**20),
    )(after(own, send), first, second, before, docs)

    came, all_keys, all_values = lax.optimization_barrier((came, all_keys, all_values))
    shares = pl.pallas_call(
        pair_kernel,
        out_shape=shape_of((heads // 2, samples // 2, deep), bf16),
        in_specs=[VMEM] * 2,
        out_specs=VMEM,
        compiler_params=params(),
        cost_estimate=cost(samples * deep, 4 * samples * deep),
    )(keep, came)
    parts = lax.all_to_all(
        after(shares, queries_here),
        "head",
        split_axis=0,
        concat_axis=0,
        tiled=True,
        axis_index_groups=[list(range(core, heads, 2)) for core in range(2)],
    )
    tiles = block // HEAD_SIZE
    run = functools.partial(attend, scale)
    first_end = CUT
    attended = run(0, first_end, low, queries_here, all_keys, all_values, across, None)
    parts, attended = lax.optimization_barrier((parts, attended))
    codes_here = code_heads.shape[2]
    stats = pl.pallas_call(
        logits_kernel,
        out_shape=shape_of((heads, 8, 128), f32),
        in_specs=[VMEM] * 5,
        out_specs=VMEM,
        compiler_params=params(),
        cost_estimate=cost(4 * samples * deep * codes_here * books, code_heads.size * 4),
    )(parts, dec_gain[None, :], code_heads, other_codes, info)
    attended = run(
        first_end,
        tiles - first_end,
        after(low, stats),
        queries_here,
        all_keys,
        all_values,
        across,
        attended,
    )
    all_stats = to_heads(stats)

    all_stats, attended = lax.optimization_barrier((all_stats, attended))
    slot_count = 2 * contexts
    placed = pl.pallas_call(
        functools.partial(place_kernel, books, samples),
        out_shape=shape_of((contexts, slot_count), f32),
        in_specs=[VMEM] * 2,
        out_specs=VMEM,
        compiler_params=params(8),
        cost_estimate=cost(10**6, 10**5),
    )(all_stats, info)
    arrived = lax.all_to_all(placed, "ctx", split_axis=0, concat_axis=0, tiled=True)
    slot_loss = jnp.sum(arrived, axis=0, keepdims=True)
    return (attended, slot_loss)


def solution(mesh):
    in_specs = (
        P(("ctx", "head"), None),
        P(("ctx", "head"), None),
        P(("ctx", "head"), None),
        P("ctx"),
        P("ctx"),
        P("ctx", None),
        P("ctx", None),
        P("head", None),
        P(),
        P(None, None, "head"),
    )
    out_specs = (P("ctx", "head"), P("ctx", None))
    return jax.shard_map(local, mesh=mesh, in_specs=in_specs, out_specs=out_specs, check_vma=False)
```

```python
import functools
import math

import jax
import jax.numpy as jnp
from jax import lax
from jax.experimental import pallas as pl
from jax.experimental.pallas import tpu as pltpu
from jax.sharding import PartitionSpec as P

HEAD_SIZE = 128
KEY_TILE = 256
CUT = 4
QUERY_TILE = 256
MASKED = -1e30
bf16 = jnp.bfloat16
f32 = jnp.float32
VMEM = pl.BlockSpec(memory_space=pltpu.VMEM)
SMEM = pl.BlockSpec(memory_space=pltpu.SMEM)
ANY = pl.BlockSpec(memory_space=pl.ANY)


def params(mib=14):
    return pltpu.CompilerParams(vmem_limit_bytes=mib * 2**20)


def cost(flops, moved, exps=0):
    return pl.CostEstimate(flops=flops, bytes_accessed=moved, transcendentals=exps)


def shape_of(shape, dtype):
    return jax.ShapeDtypeStruct(shape, dtype)


def pack_kernel(group, rows_ref, keys_hbm, values_hbm, queries_hbm, out_ref, queries_ref, sems):
    heads = out_ref.shape[0]
    frames = queries_ref.shape[0]
    per_head = rows_ref.shape[0] // heads
    copies = []
    for which, ref in enumerate((keys_hbm, values_hbm)):
        for g in range(heads):
            copies.append(
                pltpu.make_async_copy(
                    ref.at[:, pl.ds(g * HEAD_SIZE, HEAD_SIZE)],
                    out_ref.at[g, pl.ds(which * frames, frames), :],
                    sems.at[which * heads + g],
                )
            )
    pieces = []
    for p in range(4):
        span = pl.ds(p * (frames // 4), frames // 4)
        pieces.append(
            pltpu.make_async_copy(
                queries_hbm.at[span], queries_ref.at[span], sems.at[2 * heads + p]
            )
        )
    for copy in pieces + copies:
        copy.start()
    me = lax.axis_index("head")
    row = lax.broadcasted_iota(jnp.int32, (per_head, frames), 0)
    lane = lax.broadcasted_iota(jnp.int32, (per_head, frames), 1)
    wanted = jnp.full((per_head, frames), -1, jnp.int32)
    for i in range(per_head):
        wanted = jnp.where(row == i, rows_ref[me * per_head + i] - me * frames, wanted)
    chosen = jnp.where(lane == wanted, 1.0, 0.0).astype(bf16)
    for copy in pieces:
        copy.wait()
    picked = jnp.dot(chosen, queries_ref[...], preferred_element_type=f32)
    for g in range(heads):
        parts = [
            picked[:, (g * group + j) * HEAD_SIZE : (g * group + j + 1) * HEAD_SIZE]
            for j in range(group)
        ]
        out_ref[g, pl.ds(2 * frames, group * per_head), :] = jnp.concatenate(parts, axis=0).astype(
            bf16
        )
    for copy in copies:
        copy.wait()


def turned(row):
    return jnp.transpose(jnp.broadcast_to(row, (128, 128)))


def prep_kernel(
    group, rows_ref, ids_ref, owners_ref, targets_ref, docs_ref, told_ref, mine_ref, info_ref
):
    heads, frames = ids_ref.shape
    samples = rows_ref.shape[0]
    per_head = samples // heads
    docs = (ids_ref[...] + 1).astype(f32)
    docs_ref[...] = docs
    last = lax.axis_index("ctx") == lax.axis_size("ctx") - 1
    told_ref[...] = jnp.where(last, 0.0, docs)
    row = lax.broadcasted_iota(jnp.int32, (per_head, frames), 0)
    lane = lax.broadcasted_iota(jnp.int32, (per_head, frames), 1)
    for s in range(heads):
        place = jnp.zeros((per_head, frames), jnp.int32)
        for i in range(per_head):
            place = jnp.where(row == i, rows_ref[s * per_head + i] - s * frames, place)
        doc = jnp.sum(jnp.where(lane == place, docs[s : s + 1], 0.0), axis=1, keepdims=True)
        spot = ((heads + s) * frames + place).astype(f32)
        both = jnp.where(lane == 0, doc, spot)
        for j in range(group):
            mine_ref[pl.ds((s * group + j) * per_head, per_head), :] = both
    info_ref[...] = jnp.full(info_ref.shape, -1.0, f32)
    info_ref[0:1, 0:samples] = owners_ref[...].astype(f32)
    info_ref[2 : 2 + targets_ref.shape[0], 0:samples] = targets_ref[...].astype(f32)
    across = jnp.broadcast_to(info_ref[0:1, :], (128, 128))
    row = lax.broadcasted_iota(jnp.int32, (128, 128), 0)
    lane = lax.broadcasted_iota(jnp.int32, (128, 128), 1)
    same = (jnp.transpose(across) == across) & (row < lane)
    rank = jnp.sum(jnp.where(same, 1.0, 0.0), axis=0, keepdims=True)
    info_ref[1:2, :] = rank + (2 * lax.axis_index("ctx")).astype(f32)


def block_rows(s, own_ref, halo_ref, frames, which):
    heads = own_ref.shape[0]
    if s >= heads:
        return own_ref[s - heads, pl.ds(which * frames, frames), :]
    return halo_ref[pl.ds((2 * s + which) * frames, frames), :]


def window_kernel(before_ref, docs_ref, all_docs_ref, low_ref):
    docs = jnp.concatenate([before_ref[...], docs_ref[...]], axis=0)
    all_docs_ref[...] = docs
    for t in range(low_ref.shape[0]):
        first = docs_ref[t * QUERY_TILE // HEAD_SIZE : t * QUERY_TILE // HEAD_SIZE + 1, 0:1]
        below = jnp.where(docs < first, 1.0, 0.0)
        low_ref[t] = jnp.sum(below).astype(jnp.int32) // KEY_TILE


def sample_kernel(
    scale,
    own_ref,
    halo_ref,
    before_ref,
    docs_ref,
    mine_ref,
    proj_ref,
    keep_ref,
    send_ref,
    scores_ref,
):
    heads = own_ref.shape[0]
    frames = docs_ref.shape[1]
    extra = own_ref.shape[1] - 2 * frames
    group = proj_ref.shape[0] // HEAD_SIZE
    per_head = extra // group
    rows = heads * extra
    tile = 2 * frames
    queries = own_ref[:, pl.ds(2 * frames, extra), :].reshape(rows, HEAD_SIZE)
    docs = jnp.concatenate([before_ref[...], docs_ref[...]], axis=0)
    my_doc = jnp.broadcast_to(mine_ref[:, 0:1], (rows, tile))
    my_place = jnp.broadcast_to(mine_ref[:, 1:2], (rows, tile))
    lane = lax.broadcasted_iota(jnp.int32, (rows, tile), 1).astype(f32)
    highest = jnp.full((rows, HEAD_SIZE), MASKED, f32)
    for s in range(0, 2 * heads, 2):
        key_tile = jnp.concatenate(
            [block_rows(s + i, own_ref, halo_ref, frames, 0) for i in range(2)], axis=0
        )
        scores = lax.dot_general(
            queries, key_tile, (((1,), (1,)), ((), ())), preferred_element_type=f32
        )
        tile_docs = jnp.concatenate([docs[s : s + 1], docs[s + 1 : s + 2]], axis=1)
        seen = (tile_docs == my_doc) & (lane <= my_place - s * frames)
        scores = jnp.where(seen, scores * scale, MASKED)
        start = s * frames
        scores_ref[:, start : start + tile] = scores
        for part in range(tile // HEAD_SIZE):
            highest = jnp.maximum(highest, scores[:, part * HEAD_SIZE : (part + 1) * HEAD_SIZE])
    top = jnp.max(highest, axis=1, keepdims=True)
    total = jnp.zeros((rows, HEAD_SIZE), f32)
    mixed = jnp.zeros((rows, HEAD_SIZE), f32)
    for s in range(0, 2 * heads, 2):
        value_tile = jnp.concatenate(
            [block_rows(s + i, own_ref, halo_ref, frames, 1) for i in range(2)], axis=0
        )
        start = s * frames
        weights = jnp.exp2(scores_ref[:, start : start + tile] - top)
        for part in range(tile // HEAD_SIZE):
            total = total + weights[:, part * HEAD_SIZE : (part + 1) * HEAD_SIZE]
        mixed = mixed + jnp.dot(weights.astype(bf16), value_tile, preferred_element_type=f32)
    attended = mixed / jnp.sum(total, axis=1, keepdims=True)
    by_group = attended.reshape(heads, group, per_head, HEAD_SIZE)
    state = jnp.zeros((heads * per_head, proj_ref.shape[1]), f32)
    for j in range(group):
        part = by_group[:, j].reshape(heads * per_head, HEAD_SIZE).astype(bf16)
        state = state + jnp.dot(
            part, proj_ref[pl.ds(j * HEAD_SIZE, HEAD_SIZE), :], preferred_element_type=f32
        )
    rows = state.shape[0] // 2
    odd = lax.rem(lax.axis_index("head"), 2) == 1
    keep_ref[...] = jnp.where(odd, state[rows:], state[:rows])
    send_ref[...] = jnp.where(odd, state[:rows], state[rows:]).astype(bf16)


def pair_kernel(keep_ref, came_ref, out_ref):
    state = (keep_ref[...] + came_ref[...].astype(f32)).astype(bf16)
    for d in range(out_ref.shape[0]):
        out_ref[d] = state


def logits_kernel(parts_ref, gain_ref, codes_ref, other_ref, info_ref, out_ref):
    count, samples, width = parts_ref.shape
    books, _, codes = codes_ref.shape
    me = lax.axis_index("head")
    odd = lax.rem(me, 2) == 1
    other = jnp.where(odd, me - 1, me + 1)
    state = parts_ref[0].astype(f32)
    for s in range(1, count):
        state = state + parts_ref[s].astype(f32)
    square = jnp.sum(state * state, axis=1, keepdims=True)
    normed = (state * lax.rsqrt(square / width + 1e-06) * gain_ref[...]).astype(bf16)
    lane = lax.broadcasted_iota(jnp.int32, (samples, 128), 1)
    code = lax.broadcasted_iota(jnp.int32, (samples, codes), 1).astype(f32)
    stats = jnp.zeros((samples, 128), f32)
    for b in range(books):
        first = jnp.dot(normed, codes_ref[b], preferred_element_type=f32)
        second = jnp.dot(normed, other_ref[b], preferred_element_type=f32)
        top = jnp.max(jnp.maximum(first, second), axis=1, keepdims=True)
        mass = jnp.sum(jnp.exp(first - top) + jnp.exp(second - top), axis=1, keepdims=True)
        column = turned(info_ref[2 + b : 3 + b, :])
        wanted = jnp.where(odd, column[samples : 2 * samples], column[:samples])[:, 0:1]
        hit = jnp.where(code == wanted - (me * codes).astype(f32), first, 0.0)
        hit = hit + jnp.where(code == wanted - (other * codes).astype(f32), second, 0.0)
        target = jnp.sum(hit, axis=1, keepdims=True)
        for k, figure in enumerate((top, mass, target)):
            stats = jnp.where(lane == 3 * b + k, figure, stats)
    none = jnp.zeros((samples, 128), f32)
    padded = jnp.concatenate(
        [jnp.where(odd, none, stats), jnp.where(odd, stats, none), none, none], axis=0
    )
    across = jnp.transpose(padded)[:8]
    for d in range(out_ref.shape[0]):
        out_ref[d] = across


def place_kernel(books, samples, stats_ref, info_ref, out_ref):
    heads = stats_ref.shape[0]
    losses = []
    for core in range(2):
        loss = jnp.zeros((1, 128), f32)
        for b in range(books):
            tops = [stats_ref[s, 3 * b : 3 * b + 1, :] for s in range(core, heads, 2)]
            top = functools.reduce(jnp.maximum, tops)
            mass = jnp.zeros((1, 128), f32)
            target = jnp.zeros((1, 128), f32)
            for i, s in enumerate(range(core, heads, 2)):
                mass = mass + stats_ref[s, 3 * b + 1 : 3 * b + 2, :] * jnp.exp(tops[i] - top)
                target = target + stats_ref[s, 3 * b + 2 : 3 * b + 3, :]
            loss = loss + (jnp.log(mass) + top - target)
        losses.append(loss * (1.0 / books))
    lane = lax.broadcasted_iota(jnp.int32, (1, 128), 1)
    loss = jnp.where(lane < samples // 2, losses[0], losses[1])
    contexts, slots = out_ref.shape
    owner = lax.broadcasted_iota(jnp.int32, (contexts, 128), 0).astype(f32)
    spread = jnp.where(info_ref[0:1, :] == owner, loss, 0.0)
    column = lax.broadcasted_iota(jnp.int32, (128, 128), 1).astype(f32)
    column = jnp.where(turned(info_ref[1:2, :]) == column, 1.0, 0.0)[:, :slots]
    out_ref[...] = jnp.dot(
        spread, column, preferred_element_type=f32, precision=lax.Precision.HIGHEST
    )


def main_kernel(scale, first_tile, steps, low_ref, queries_ref, own_ref, halo_ref, across_ref, *refs):
    out_ref, bias_ref, scores_ref, keys_ref, values_ref = refs[-5:]
    tile, width = queries_ref.shape
    group = width // HEAD_SIZE
    parts = tile // HEAD_SIZE
    block = keys_ref.shape[0] // 2
    number = first_tile + pl.program_id(0)
    start = block + number * tile
    low = low_ref[number]
    high = (start + tile + KEY_TILE - 1) // KEY_TILE
    halves = KEY_TILE // HEAD_SIZE
    units = [(j, r) for j in range(group) for r in range(parts)]
    frames = HEAD_SIZE
    sources = 2 * block // frames
    first_source = first_tile * parts
    last_source = sources // 2 + (first_tile + steps) * parts

    @pl.when(pl.program_id(0) == 0)
    def _():
        for s in range(first_source, last_source):
            rows = pl.ds(s * frames, frames)
            keys_ref[rows, :] = block_rows(s, own_ref, halo_ref, frames, 0)
            values_ref[rows, :] = block_rows(s, own_ref, halo_ref, frames, 1)


    def body(count):
        base = pl.multiple_of(low * KEY_TILE, KEY_TILE)
        ahead = lax.broadcasted_iota(jnp.int32, (HEAD_SIZE, HEAD_SIZE), 0) - lax.broadcasted_iota(
            jnp.int32, (HEAD_SIZE, HEAD_SIZE), 1
        )
        for r in range(parts):
            row = (block + number * tile) // HEAD_SIZE + r
            my_doc = turned(across_ref[pl.ds(row, 1), :])
            for k in range(count * halves):
                doc = across_ref[pl.ds(low * halves + k, 1), :]
                seen = (doc == my_doc) & (ahead >= base + k * HEAD_SIZE - start - r * HEAD_SIZE)
                bias_ref[r, :, k * HEAD_SIZE : (k + 1) * HEAD_SIZE] = jnp.where(seen, 0.0, MASKED)
        tops = []
        for u, (j, r) in enumerate(units):
            queries = queries_ref[r * HEAD_SIZE : (r + 1) * HEAD_SIZE, j * HEAD_SIZE : (j + 1) * HEAD_SIZE]
            highest = None
            for k in range(count):
                span = slice(k * KEY_TILE, (k + 1) * KEY_TILE)
                key_tile = keys_ref[pl.ds(base + k * KEY_TILE, KEY_TILE), :]
                scores = lax.dot_general(
                    queries, key_tile, (((1,), (1,)), ((), ())), preferred_element_type=f32
                )
                scores = scores * scale + bias_ref[r, :, span]
                scores_ref[u, :, span] = scores
                most = jnp.maximum(scores[:, :HEAD_SIZE], scores[:, HEAD_SIZE:])
                highest = most if highest is None else jnp.maximum(highest, most)
            tops.append(jnp.max(highest, axis=1, keepdims=True))
        one = jnp.ones((count * KEY_TILE, HEAD_SIZE), bf16)
        value_rows = jnp.concatenate([values_ref[pl.ds(base, count * KEY_TILE), :], one], axis=1)
        for u, (j, r) in enumerate(units):
            weights = jnp.concatenate(
                [
                    jnp.exp2(scores_ref[u, :, k * KEY_TILE : (k + 1) * KEY_TILE] - tops[u]).astype(bf16)
                    for k in range(count)
                ],
                axis=1,
            )
            mixed = jnp.dot(weights, value_rows, preferred_element_type=f32)
            out_ref[r * HEAD_SIZE : (r + 1) * HEAD_SIZE, j * HEAD_SIZE : (j + 1) * HEAD_SIZE] = (
                mixed[:, :HEAD_SIZE] / mixed[:, HEAD_SIZE:]
            ).astype(bf16)

    most = scores_ref.shape[2] // KEY_TILE
    for count in range(1, most + 1):
        pl.when(high - low == count)(functools.partial(body, count))


def attend(scale, first_tile, tiles, low, queries, own, halo, across, before):
    block, width = queries.shape
    tile = QUERY_TILE
    first_tile, tiles = first_tile * HEAD_SIZE // tile, tiles * HEAD_SIZE // tile
    group = width // HEAD_SIZE
    most = (block + tile + KEY_TILE - 1) // KEY_TILE
    rows = lambda i: (first_tile + i, 0)
    whole = lambda i: (0, 0)
    in_specs = [
        SMEM,
        pl.BlockSpec((tile, width), rows),
        pl.BlockSpec(own.shape, lambda i: (0, 0, 0)),
        pl.BlockSpec(halo.shape, whole),
        pl.BlockSpec(across.shape, whole),
    ]
    operands = [low, queries, own, halo, across]
    aliases = {}
    if before is not None:
        in_specs.append(pl.BlockSpec(memory_space=pl.ANY))
        operands.append(before)
        aliases = {len(operands) - 1: 0}
    pairs = tiles * group * tile * 4 * KEY_TILE
    return pl.pallas_call(
        functools.partial(main_kernel, scale, first_tile, tiles),
        grid=(tiles,),
        out_shape=shape_of((block, width), bf16),
        in_specs=in_specs,
        out_specs=pl.BlockSpec((tile, width), rows),
        scratch_shapes=[
            pltpu.VMEM((tile // HEAD_SIZE, HEAD_SIZE, most * KEY_TILE), f32),
            pltpu.VMEM((group * tile // HEAD_SIZE, HEAD_SIZE, most * KEY_TILE), f32),
            pltpu.VMEM((2 * block, HEAD_SIZE), bf16),
            pltpu.VMEM((2 * block, HEAD_SIZE), bf16),
        ],
        input_output_aliases=aliases,
        compiler_params=params(),
        cost_estimate=cost(pairs * 6 * HEAD_SIZE, 2 * 2**20, pairs),
    )(*operands)


def to_heads(value):
    return lax.all_to_all(value, "head", split_axis=0, concat_axis=0, tiled=True)


def after(value, *others):
    return lax.optimization_barrier((value, *others))[0]


def local(
    queries, keys, values, doc_ids, sample_rows, owners, targets, in_proj, dec_gain, code_heads
):
    heads = lax.axis_size("head")
    contexts = lax.axis_size("ctx")
    head_number = lax.axis_index("head")
    ctx_number = lax.axis_index("ctx")
    frames = keys.shape[0]
    block = doc_ids.shape[0]
    samples = sample_rows.shape[0]
    per_head = samples // heads
    width = queries.shape[1] // heads
    group = width // HEAD_SIZE
    scale = math.log2(math.e) / math.sqrt(HEAD_SIZE)
    deep = in_proj.shape[1]
    books = targets.shape[1]

    packed = pl.pallas_call(
        functools.partial(pack_kernel, group),
        out_shape=shape_of((heads, 2 * frames + group * per_head, HEAD_SIZE), bf16),
        in_specs=[SMEM, ANY, ANY, ANY],
        out_specs=VMEM,
        scratch_shapes=[
            pltpu.VMEM(queries.shape, bf16),
            pltpu.SemaphoreType.DMA((2 * heads + 4,)),
        ],
        compiler_params=params(56),
        cost_estimate=cost(2 * per_head * frames * queries.shape[1], 2 * 2**20),
    )(sample_rows, keys, values, queries)
    own = to_heads(packed)

    docs, told, mine, info = pl.pallas_call(
        functools.partial(prep_kernel, group),
        out_shape=(
            shape_of((heads, frames), f32),
            shape_of((heads, frames), f32),
            shape_of((samples * group, 128), f32),
            shape_of((8, 128), f32),
        ),
        in_specs=[SMEM, VMEM, VMEM, VMEM],
        out_specs=(VMEM,) * 4,
        compiler_params=params(8),
        cost_estimate=cost(10**6, 4 * 10**5),
    )(
        after(sample_rows, packed),
        doc_ids.reshape(heads, frames),
        owners.reshape(1, samples),
        targets.T,
    )
    ring = [(s, (s + 1) % contexts) for s in range(contexts)]
    before = lax.ppermute(told, "ctx", ring)
    by_head = jnp.transpose(after(queries, packed).reshape(frames, heads, width), (1, 0, 2))
    own, docs, mine, before, by_head = lax.optimization_barrier((own, docs, mine, before, by_head))
    halo = lax.ppermute(own[:, : 2 * frames].reshape(2 * block, HEAD_SIZE), "ctx", ring)
    queries_here = to_heads(by_head).reshape(block, width)
    pairs = [(s, s + 1 - 2 * (s % 2)) for s in range(heads)]
    other_codes = lax.ppermute(after(code_heads, own), "head", pairs)

    across, low = pl.pallas_call(
        window_kernel,
        out_shape=(
            shape_of((2 * heads, frames), f32),
            shape_of((block // QUERY_TILE,), jnp.int32),
        ),
        in_specs=[VMEM] * 2,
        out_specs=(VMEM, SMEM),
        compiler_params=params(8),
        cost_estimate=cost(0, 2 * 2**16),
    )(before, docs)
    halo, across, low = lax.optimization_barrier((halo, across, low))
    keep, send = pl.pallas_call(
        functools.partial(sample_kernel, scale),
        out_shape=(shape_of((samples // 2, deep), f32), shape_of((samples // 2, deep), bf16)),
        in_specs=[VMEM] * 6,
        out_specs=(VMEM, VMEM),
        scratch_shapes=[pltpu.VMEM((samples * group, 2 * block), f32)],
        compiler_params=params(),
        cost_estimate=cost(
            240 * samples * group * 2 * block * HEAD_SIZE, 4 * 2**20, samples * group * 2 * block
        ),
    )(own, halo, before, docs, mine, in_proj)
    came = lax.ppermute(send, "head", pairs)

    shares = pl.pallas_call(
        pair_kernel,
        out_shape=shape_of((heads // 2, samples // 2, deep), bf16),
        in_specs=[VMEM] * 2,
        out_specs=VMEM,
        compiler_params=params(),
        cost_estimate=cost(samples * deep, 4 * samples * deep),
    )(keep, came)
    parts = lax.all_to_all(
        after(shares, queries_here),
        "head",
        split_axis=0,
        concat_axis=0,
        tiled=True,
        axis_index_groups=[list(range(core, heads, 2)) for core in range(2)],
    )
    tiles = block // HEAD_SIZE
    run = functools.partial(attend, scale)
    first_end = CUT
    attended = run(0, first_end, low, queries_here, own, halo, across, None)
    parts, attended = lax.optimization_barrier((parts, attended))
    codes_here = code_heads.shape[2]
    stats = pl.pallas_call(
        logits_kernel,
        out_shape=shape_of((heads, 8, 128), f32),
        in_specs=[VMEM] * 5,
        out_specs=VMEM,
        compiler_params=params(),
        cost_estimate=cost(4 * samples * deep * codes_here * books, code_heads.size * 4),
    )(parts, dec_gain[None, :], code_heads, other_codes, info)
    attended = run(
        first_end,
        tiles - first_end,
        after(low, stats),
        queries_here,
        own,
        halo,
        across,
        attended,
    )
    all_stats = to_heads(stats)

    all_stats, attended = lax.optimization_barrier((all_stats, attended))
    slot_count = 2 * contexts
    placed = pl.pallas_call(
        functools.partial(place_kernel, books, samples),
        out_shape=shape_of((contexts, slot_count), f32),
        in_specs=[VMEM] * 2,
        out_specs=VMEM,
        compiler_params=params(8),
        cost_estimate=cost(10**6, 10**5),
    )(all_stats, info)
    arrived = lax.all_to_all(placed, "ctx", split_axis=0, concat_axis=0, tiled=True)
    slot_loss = jnp.sum(arrived, axis=0, keepdims=True)
    return (attended, slot_loss)


def solution(mesh):
    in_specs = (
        P(("ctx", "head"), None),
        P(("ctx", "head"), None),
        P(("ctx", "head"), None),
        P("ctx"),
        P("ctx"),
        P("ctx", None),
        P("ctx", None),
        P("head", None),
        P(),
        P(None, None, "head"),
    )
    out_specs = (P("ctx", "head"), P("ctx", None))
    return jax.shard_map(local, mesh=mesh, in_specs=in_specs, out_specs=out_specs, check_vma=False)
```

```python
import functools
import math

import jax
import jax.numpy as jnp
from jax import lax
from jax.experimental import pallas as pl
from jax.experimental.pallas import tpu as pltpu
from jax.sharding import PartitionSpec as P

HEAD_SIZE = 128
KEY_TILE = 256
CUT = 4
QUERY_TILE = 256
MASKED = -1e30
bf16 = jnp.bfloat16
f32 = jnp.float32
VMEM = pl.BlockSpec(memory_space=pltpu.VMEM)
SMEM = pl.BlockSpec(memory_space=pltpu.SMEM)
ANY = pl.BlockSpec(memory_space=pl.ANY)


def params(mib=14):
    return pltpu.CompilerParams(vmem_limit_bytes=mib * 2**20)


def cost(flops, moved, exps=0):
    return pl.CostEstimate(flops=flops, bytes_accessed=moved, transcendentals=exps)


def shape_of(shape, dtype):
    return jax.ShapeDtypeStruct(shape, dtype)


def pack_kernel(group, rows_ref, keys_hbm, values_hbm, queries_hbm, out_ref, queries_ref, sems):
    heads = out_ref.shape[0]
    frames = queries_ref.shape[0]
    per_head = rows_ref.shape[0] // heads
    copies = []
    for which, ref in enumerate((keys_hbm, values_hbm)):
        for g in range(heads):
            copies.append(
                pltpu.make_async_copy(
                    ref.at[:, pl.ds(g * HEAD_SIZE, HEAD_SIZE)],
                    out_ref.at[g, pl.ds(which * frames, frames), :],
                    sems.at[which * heads + g],
                )
            )
    pieces = []
    for p in range(4):
        span = pl.ds(p * (frames // 4), frames // 4)
        pieces.append(
            pltpu.make_async_copy(
                queries_hbm.at[span], queries_ref.at[span], sems.at[2 * heads + p]
            )
        )
    for copy in pieces + copies:
        copy.start()
    me = lax.axis_index("head")
    row = lax.broadcasted_iota(jnp.int32, (per_head, frames), 0)
    lane = lax.broadcasted_iota(jnp.int32, (per_head, frames), 1)
    wanted = jnp.full((per_head, frames), -1, jnp.int32)
    for i in range(per_head):
        wanted = jnp.where(row == i, rows_ref[me * per_head + i] - me * frames, wanted)
    chosen = jnp.where(lane == wanted, 1.0, 0.0).astype(bf16)
    for copy in pieces:
        copy.wait()
    picked = jnp.dot(chosen, queries_ref[...], preferred_element_type=f32)
    for g in range(heads):
        parts = [
            picked[:, (g * group + j) * HEAD_SIZE : (g * group + j + 1) * HEAD_SIZE]
            for j in range(group)
        ]
        out_ref[g, pl.ds(2 * frames, group * per_head), :] = jnp.concatenate(parts, axis=0).astype(
            bf16
        )
    for copy in copies:
        copy.wait()


def turned(row):
    return jnp.transpose(jnp.broadcast_to(row, (128, 128)))


def prep_kernel(
    group, rows_ref, ids_ref, owners_ref, targets_ref, docs_ref, told_ref, mine_ref, info_ref
):
    heads, frames = ids_ref.shape
    samples = rows_ref.shape[0]
    per_head = samples // heads
    docs = (ids_ref[...] + 1).astype(f32)
    docs_ref[...] = docs
    last = lax.axis_index("ctx") == lax.axis_size("ctx") - 1
    told_ref[...] = jnp.where(last, 0.0, docs)
    row = lax.broadcasted_iota(jnp.int32, (per_head, frames), 0)
    lane = lax.broadcasted_iota(jnp.int32, (per_head, frames), 1)
    for s in range(heads):
        place = jnp.zeros((per_head, frames), jnp.int32)
        for i in range(per_head):
            place = jnp.where(row == i, rows_ref[s * per_head + i] - s * frames, place)
        doc = jnp.sum(jnp.where(lane == place, docs[s : s + 1], 0.0), axis=1, keepdims=True)
        spot = ((heads + s) * frames + place).astype(f32)
        both = jnp.where(lane == 0, doc, spot)
        for j in range(group):
            mine_ref[pl.ds((s * group + j) * per_head, per_head), :] = both
    info_ref[...] = jnp.full(info_ref.shape, -1.0, f32)
    info_ref[0:1, 0:samples] = owners_ref[...].astype(f32)
    info_ref[2 : 2 + targets_ref.shape[0], 0:samples] = targets_ref[...].astype(f32)
    across = jnp.broadcast_to(info_ref[0:1, :], (128, 128))
    row = lax.broadcasted_iota(jnp.int32, (128, 128), 0)
    lane = lax.broadcasted_iota(jnp.int32, (128, 128), 1)
    same = (jnp.transpose(across) == across) & (row < lane)
    rank = jnp.sum(jnp.where(same, 1.0, 0.0), axis=0, keepdims=True)
    info_ref[1:2, :] = rank + (2 * lax.axis_index("ctx")).astype(f32)


def block_rows(s, own_ref, halo_ref, frames, which):
    heads = own_ref.shape[0]
    if s >= heads:
        return own_ref[s - heads, pl.ds(which * frames, frames), :]
    return halo_ref[pl.ds((2 * s + which) * frames, frames), :]


def window_kernel(before_ref, docs_ref, proj_hbm, all_docs_ref, low_ref, proj_ref, sem):
    fetch = pltpu.make_async_copy(proj_hbm, proj_ref, sem)
    fetch.start()
    docs = jnp.concatenate([before_ref[...], docs_ref[...]], axis=0)
    all_docs_ref[...] = docs
    for t in range(low_ref.shape[0]):
        first = docs_ref[t * QUERY_TILE // HEAD_SIZE : t * QUERY_TILE // HEAD_SIZE + 1, 0:1]
        below = jnp.where(docs < first, 1.0, 0.0)
        low_ref[t] = jnp.sum(below).astype(jnp.int32) // KEY_TILE
    fetch.wait()


def sample_kernel(
    scale,
    own_ref,
    halo_ref,
    before_ref,
    docs_ref,
    mine_ref,
    proj_ref,
    keep_ref,
    send_ref,
    scores_ref,
):
    heads = own_ref.shape[0]
    frames = docs_ref.shape[1]
    extra = own_ref.shape[1] - 2 * frames
    group = proj_ref.shape[0] // HEAD_SIZE
    per_head = extra // group
    rows = heads * extra
    tile = 2 * frames
    queries = own_ref[:, pl.ds(2 * frames, extra), :].reshape(rows, HEAD_SIZE)
    docs = jnp.concatenate([before_ref[...], docs_ref[...]], axis=0)
    my_doc = jnp.broadcast_to(mine_ref[:, 0:1], (rows, tile))
    my_place = jnp.broadcast_to(mine_ref[:, 1:2], (rows, tile))
    lane = lax.broadcasted_iota(jnp.int32, (rows, tile), 1).astype(f32)
    highest = jnp.full((rows, HEAD_SIZE), MASKED, f32)
    for s in range(0, 2 * heads, 2):
        key_tile = jnp.concatenate(
            [block_rows(s + i, own_ref, halo_ref, frames, 0) for i in range(2)], axis=0
        )
        scores = lax.dot_general(
            queries, key_tile, (((1,), (1,)), ((), ())), preferred_element_type=f32
        )
        tile_docs = jnp.concatenate([docs[s : s + 1], docs[s + 1 : s + 2]], axis=1)
        seen = (tile_docs == my_doc) & (lane <= my_place - s * frames)
        scores = jnp.where(seen, scores * scale, MASKED)
        start = s * frames
        scores_ref[:, start : start + tile] = scores
        for part in range(tile // HEAD_SIZE):
            highest = jnp.maximum(highest, scores[:, part * HEAD_SIZE : (part + 1) * HEAD_SIZE])
    top = jnp.max(highest, axis=1, keepdims=True)
    total = jnp.zeros((rows, HEAD_SIZE), f32)
    mixed = jnp.zeros((rows, HEAD_SIZE), f32)
    for s in range(0, 2 * heads, 2):
        value_tile = jnp.concatenate(
            [block_rows(s + i, own_ref, halo_ref, frames, 1) for i in range(2)], axis=0
        )
        start = s * frames
        weights = jnp.exp2(scores_ref[:, start : start + tile] - top)
        for part in range(tile // HEAD_SIZE):
            total = total + weights[:, part * HEAD_SIZE : (part + 1) * HEAD_SIZE]
        mixed = mixed + jnp.dot(weights.astype(bf16), value_tile, preferred_element_type=f32)
    attended = mixed / jnp.sum(total, axis=1, keepdims=True)
    by_group = attended.reshape(heads, group, per_head, HEAD_SIZE)
    state = jnp.zeros((heads * per_head, proj_ref.shape[1]), f32)
    for j in range(group):
        part = by_group[:, j].reshape(heads * per_head, HEAD_SIZE).astype(bf16)
        state = state + jnp.dot(
            part, proj_ref[pl.ds(j * HEAD_SIZE, HEAD_SIZE), :], preferred_element_type=f32
        )
    rows = state.shape[0] // 2
    odd = lax.rem(lax.axis_index("head"), 2) == 1
    keep_ref[...] = jnp.where(odd, state[rows:], state[:rows])
    send_ref[...] = jnp.where(odd, state[:rows], state[rows:]).astype(bf16)


def pair_kernel(keep_ref, came_ref, out_ref):
    state = (keep_ref[...] + came_ref[...].astype(f32)).astype(bf16)
    for d in range(out_ref.shape[0]):
        out_ref[d] = state


def logits_kernel(parts_ref, gain_ref, codes_ref, other_ref, info_ref, out_ref):
    count, samples, width = parts_ref.shape
    books, _, codes = codes_ref.shape
    me = lax.axis_index("head")
    odd = lax.rem(me, 2) == 1
    other = jnp.where(odd, me - 1, me + 1)
    state = parts_ref[0].astype(f32)
    for s in range(1, count):
        state = state + parts_ref[s].astype(f32)
    square = jnp.sum(state * state, axis=1, keepdims=True)
    normed = (state * lax.rsqrt(square / width + 1e-06) * gain_ref[...]).astype(bf16)
    lane = lax.broadcasted_iota(jnp.int32, (samples, 128), 1)
    code = lax.broadcasted_iota(jnp.int32, (samples, codes), 1).astype(f32)
    stats = jnp.zeros((samples, 128), f32)
    for b in range(books):
        first = jnp.dot(normed, codes_ref[b], preferred_element_type=f32)
        second = jnp.dot(normed, other_ref[b], preferred_element_type=f32)
        top = jnp.max(jnp.maximum(first, second), axis=1, keepdims=True)
        mass = jnp.sum(jnp.exp(first - top) + jnp.exp(second - top), axis=1, keepdims=True)
        column = turned(info_ref[2 + b : 3 + b, :])
        wanted = jnp.where(odd, column[samples : 2 * samples], column[:samples])[:, 0:1]
        hit = jnp.where(code == wanted - (me * codes).astype(f32), first, 0.0)
        hit = hit + jnp.where(code == wanted - (other * codes).astype(f32), second, 0.0)
        target = jnp.sum(hit, axis=1, keepdims=True)
        for k, figure in enumerate((top, mass, target)):
            stats = jnp.where(lane == 3 * b + k, figure, stats)
    none = jnp.zeros((samples, 128), f32)
    padded = jnp.concatenate(
        [jnp.where(odd, none, stats), jnp.where(odd, stats, none), none, none], axis=0
    )
    across = jnp.transpose(padded)[:8]
    for d in range(out_ref.shape[0]):
        out_ref[d] = across


def place_kernel(books, samples, stats_ref, info_ref, out_ref):
    heads = stats_ref.shape[0]
    losses = []
    for core in range(2):
        loss = jnp.zeros((1, 128), f32)
        for b in range(books):
            tops = [stats_ref[s, 3 * b : 3 * b + 1, :] for s in range(core, heads, 2)]
            top = functools.reduce(jnp.maximum, tops)
            mass = jnp.zeros((1, 128), f32)
            target = jnp.zeros((1, 128), f32)
            for i, s in enumerate(range(core, heads, 2)):
                mass = mass + stats_ref[s, 3 * b + 1 : 3 * b + 2, :] * jnp.exp(tops[i] - top)
                target = target + stats_ref[s, 3 * b + 2 : 3 * b + 3, :]
            loss = loss + (jnp.log(mass) + top - target)
        losses.append(loss * (1.0 / books))
    lane = lax.broadcasted_iota(jnp.int32, (1, 128), 1)
    loss = jnp.where(lane < samples // 2, losses[0], losses[1])
    contexts, slots = out_ref.shape
    owner = lax.broadcasted_iota(jnp.int32, (contexts, 128), 0).astype(f32)
    spread = jnp.where(info_ref[0:1, :] == owner, loss, 0.0)
    column = lax.broadcasted_iota(jnp.int32, (128, 128), 1).astype(f32)
    column = jnp.where(turned(info_ref[1:2, :]) == column, 1.0, 0.0)[:, :slots]
    out_ref[...] = jnp.dot(
        spread, column, preferred_element_type=f32, precision=lax.Precision.HIGHEST
    )


def main_kernel(scale, first_tile, steps, low_ref, queries_ref, own_ref, halo_ref, across_ref, *refs):
    out_ref, bias_ref, scores_ref, keys_ref, values_ref = refs[-5:]
    tile, width = queries_ref.shape
    group = width // HEAD_SIZE
    parts = tile // HEAD_SIZE
    block = keys_ref.shape[0] // 2
    number = first_tile + pl.program_id(0)
    start = block + number * tile
    low = low_ref[number]
    high = (start + tile + KEY_TILE - 1) // KEY_TILE
    halves = KEY_TILE // HEAD_SIZE
    units = [(j, r) for j in range(group) for r in range(parts)]
    frames = HEAD_SIZE
    sources = 2 * block // frames
    first_source = first_tile * parts
    last_source = sources // 2 + (first_tile + steps) * parts

    @pl.when(pl.program_id(0) == 0)
    def _():
        for s in range(first_source, last_source):
            rows = pl.ds(s * frames, frames)
            keys_ref[rows, :] = block_rows(s, own_ref, halo_ref, frames, 0)
            values_ref[rows, :] = block_rows(s, own_ref, halo_ref, frames, 1)


    def body(count):
        base = pl.multiple_of(low * KEY_TILE, KEY_TILE)
        ahead = lax.broadcasted_iota(jnp.int32, (HEAD_SIZE, HEAD_SIZE), 0) - lax.broadcasted_iota(
            jnp.int32, (HEAD_SIZE, HEAD_SIZE), 1
        )
        for r in range(parts):
            row = (block + number * tile) // HEAD_SIZE + r
            my_doc = turned(across_ref[pl.ds(row, 1), :])
            for k in range(count * halves):
                doc = across_ref[pl.ds(low * halves + k, 1), :]
                seen = (doc == my_doc) & (ahead >= base + k * HEAD_SIZE - start - r * HEAD_SIZE)
                bias_ref[r, :, k * HEAD_SIZE : (k + 1) * HEAD_SIZE] = jnp.where(seen, 0.0, MASKED)
        tops = []
        for u, (j, r) in enumerate(units):
            queries = queries_ref[r * HEAD_SIZE : (r + 1) * HEAD_SIZE, j * HEAD_SIZE : (j + 1) * HEAD_SIZE]
            highest = None
            for k in range(count):
                span = slice(k * KEY_TILE, (k + 1) * KEY_TILE)
                key_tile = keys_ref[pl.ds(base + k * KEY_TILE, KEY_TILE), :]
                scores = lax.dot_general(
                    queries, key_tile, (((1,), (1,)), ((), ())), preferred_element_type=f32
                )
                scores = scores * scale + bias_ref[r, :, span]
                scores_ref[u, :, span] = scores
                most = jnp.maximum(scores[:, :HEAD_SIZE], scores[:, HEAD_SIZE:])
                highest = most if highest is None else jnp.maximum(highest, most)
            tops.append(jnp.max(highest, axis=1, keepdims=True))
        one = jnp.ones((count * KEY_TILE, HEAD_SIZE), bf16)
        value_rows = jnp.concatenate([values_ref[pl.ds(base, count * KEY_TILE), :], one], axis=1)
        for u, (j, r) in enumerate(units):
            weights = jnp.concatenate(
                [
                    jnp.exp2(scores_ref[u, :, k * KEY_TILE : (k + 1) * KEY_TILE] - tops[u]).astype(bf16)
                    for k in range(count)
                ],
                axis=1,
            )
            mixed = jnp.dot(weights, value_rows, preferred_element_type=f32)
            out_ref[r * HEAD_SIZE : (r + 1) * HEAD_SIZE, j * HEAD_SIZE : (j + 1) * HEAD_SIZE] = (
                mixed[:, :HEAD_SIZE] / mixed[:, HEAD_SIZE:]
            ).astype(bf16)

    most = scores_ref.shape[2] // KEY_TILE
    for count in range(1, most + 1):
        pl.when(high - low == count)(functools.partial(body, count))


def attend(scale, first_tile, tiles, low, queries, own, halo, across, before):
    block, width = queries.shape
    tile = QUERY_TILE
    first_tile, tiles = first_tile * HEAD_SIZE // tile, tiles * HEAD_SIZE // tile
    group = width // HEAD_SIZE
    most = (block + tile + KEY_TILE - 1) // KEY_TILE
    rows = lambda i: (first_tile + i, 0)
    whole = lambda i: (0, 0)
    in_specs = [
        SMEM,
        pl.BlockSpec((tile, width), rows),
        pl.BlockSpec(own.shape, lambda i: (0, 0, 0)),
        pl.BlockSpec(halo.shape, whole),
        pl.BlockSpec(across.shape, whole),
    ]
    operands = [low, queries, own, halo, across]
    aliases = {}
    if before is not None:
        in_specs.append(pl.BlockSpec(memory_space=pl.ANY))
        operands.append(before)
        aliases = {len(operands) - 1: 0}
    pairs = tiles * group * tile * 4 * KEY_TILE
    return pl.pallas_call(
        functools.partial(main_kernel, scale, first_tile, tiles),
        grid=(tiles,),
        out_shape=shape_of((block, width), bf16),
        in_specs=in_specs,
        out_specs=pl.BlockSpec((tile, width), rows),
        scratch_shapes=[
            pltpu.VMEM((tile // HEAD_SIZE, HEAD_SIZE, most * KEY_TILE), f32),
            pltpu.VMEM((group * tile // HEAD_SIZE, HEAD_SIZE, most * KEY_TILE), f32),
            pltpu.VMEM((2 * block, HEAD_SIZE), bf16),
            pltpu.VMEM((2 * block, HEAD_SIZE), bf16),
        ],
        input_output_aliases=aliases,
        compiler_params=params(),
        cost_estimate=cost(pairs * 6 * HEAD_SIZE, 2 * 2**20, pairs),
    )(*operands)


def to_heads(value):
    return lax.all_to_all(value, "head", split_axis=0, concat_axis=0, tiled=True)


def after(value, *others):
    return lax.optimization_barrier((value, *others))[0]


def local(
    queries, keys, values, doc_ids, sample_rows, owners, targets, in_proj, dec_gain, code_heads
):
    heads = lax.axis_size("head")
    contexts = lax.axis_size("ctx")
    head_number = lax.axis_index("head")
    ctx_number = lax.axis_index("ctx")
    frames = keys.shape[0]
    block = doc_ids.shape[0]
    samples = sample_rows.shape[0]
    per_head = samples // heads
    width = queries.shape[1] // heads
    group = width // HEAD_SIZE
    scale = math.log2(math.e) / math.sqrt(HEAD_SIZE)
    deep = in_proj.shape[1]
    books = targets.shape[1]

    packed = pl.pallas_call(
        functools.partial(pack_kernel, group),
        out_shape=shape_of((heads, 2 * frames + group * per_head, HEAD_SIZE), bf16),
        in_specs=[SMEM, ANY, ANY, ANY],
        out_specs=VMEM,
        scratch_shapes=[
            pltpu.VMEM(queries.shape, bf16),
            pltpu.SemaphoreType.DMA((2 * heads + 4,)),
        ],
        compiler_params=params(56),
        cost_estimate=cost(2 * per_head * frames * queries.shape[1], 2 * 2**20),
    )(sample_rows, keys, values, queries)
    own = to_heads(packed)

    docs, told, mine, info = pl.pallas_call(
        functools.partial(prep_kernel, group),
        out_shape=(
            shape_of((heads, frames), f32),
            shape_of((heads, frames), f32),
            shape_of((samples * group, 128), f32),
            shape_of((8, 128), f32),
        ),
        in_specs=[SMEM, VMEM, VMEM, VMEM],
        out_specs=(VMEM,) * 4,
        compiler_params=params(8),
        cost_estimate=cost(10**6, 4 * 10**5),
    )(
        after(sample_rows, packed),
        doc_ids.reshape(heads, frames),
        owners.reshape(1, samples),
        targets.T,
    )
    ring = [(s, (s + 1) % contexts) for s in range(contexts)]
    before = lax.ppermute(told, "ctx", ring)
    by_head = jnp.transpose(after(queries, packed).reshape(frames, heads, width), (1, 0, 2))
    own, docs, mine, before, by_head = lax.optimization_barrier((own, docs, mine, before, by_head))
    halo = lax.ppermute(own[:, : 2 * frames].reshape(2 * block, HEAD_SIZE), "ctx", ring)
    queries_here = to_heads(by_head).reshape(block, width)
    pairs = [(s, s + 1 - 2 * (s % 2)) for s in range(heads)]
    other_codes = lax.ppermute(after(code_heads, own), "head", pairs)

    across, low, proj_here = pl.pallas_call(
        window_kernel,
        out_shape=(
            shape_of((2 * heads, frames), f32),
            shape_of((block // QUERY_TILE,), jnp.int32),
            shape_of(in_proj.shape, bf16),
        ),
        in_specs=[VMEM, VMEM, ANY],
        out_specs=(VMEM, SMEM, VMEM),
        scratch_shapes=[pltpu.SemaphoreType.DMA],
        compiler_params=params(8),
        cost_estimate=cost(0, 2 * 2**16),
    )(before, docs, after(in_proj, own))
    halo, across, low, proj_here = lax.optimization_barrier((halo, across, low, proj_here))
    keep, send = pl.pallas_call(
        functools.partial(sample_kernel, scale),
        out_shape=(shape_of((samples // 2, deep), f32), shape_of((samples // 2, deep), bf16)),
        in_specs=[VMEM] * 6,
        out_specs=(VMEM, VMEM),
        scratch_shapes=[pltpu.VMEM((samples * group, 2 * block), f32)],
        compiler_params=params(),
        cost_estimate=cost(
            240 * samples * group * 2 * block * HEAD_SIZE, 4 * 2**20, samples * group * 2 * block
        ),
    )(own, halo, before, docs, mine, proj_here)
    came = lax.ppermute(send, "head", pairs)

    shares = pl.pallas_call(
        pair_kernel,
        out_shape=shape_of((heads // 2, samples // 2, deep), bf16),
        in_specs=[VMEM] * 2,
        out_specs=VMEM,
        compiler_params=params(),
        cost_estimate=cost(samples * deep, 4 * samples * deep),
    )(keep, came)
    parts = lax.all_to_all(
        after(shares, queries_here),
        "head",
        split_axis=0,
        concat_axis=0,
        tiled=True,
        axis_index_groups=[list(range(core, heads, 2)) for core in range(2)],
    )
    tiles = block // HEAD_SIZE
    run = functools.partial(attend, scale)
    first_end = CUT
    attended = run(0, first_end, low, queries_here, own, halo, across, None)
    parts, attended = lax.optimization_barrier((parts, attended))
    codes_here = code_heads.shape[2]
    stats = pl.pallas_call(
        logits_kernel,
        out_shape=shape_of((heads, 8, 128), f32),
        in_specs=[VMEM] * 5,
        out_specs=VMEM,
        compiler_params=params(),
        cost_estimate=cost(4 * samples * deep * codes_here * books, code_heads.size * 4),
    )(parts, dec_gain[None, :], code_heads, other_codes, info)
    attended = run(
        first_end,
        tiles - first_end,
        after(low, stats),
        queries_here,
        own,
        halo,
        across,
        attended,
    )
    all_stats = to_heads(stats)

    all_stats, attended = lax.optimization_barrier((all_stats, attended))
    slot_count = 2 * contexts
    placed = pl.pallas_call(
        functools.partial(place_kernel, books, samples),
        out_shape=shape_of((contexts, slot_count), f32),
        in_specs=[VMEM] * 2,
        out_specs=VMEM,
        compiler_params=params(8),
        cost_estimate=cost(10**6, 10**5),
    )(all_stats, info)
    arrived = lax.all_to_all(placed, "ctx", split_axis=0, concat_axis=0, tiled=True)
    slot_loss = jnp.sum(arrived, axis=0, keepdims=True)
    return (attended, slot_loss)


def solution(mesh):
    in_specs = (
        P(("ctx", "head"), None),
        P(("ctx", "head"), None),
        P(("ctx", "head"), None),
        P("ctx"),
        P("ctx"),
        P("ctx", None),
        P("ctx", None),
        P("head", None),
        P(),
        P(None, None, "head"),
    )
    out_specs = (P("ctx", "head"), P("ctx", None))
    return jax.shard_map(local, mesh=mesh, in_specs=in_specs, out_specs=out_specs, check_vma=False)
```

```python
import functools
import math

import jax
import jax.numpy as jnp
from jax import lax
from jax.experimental import pallas as pl
from jax.experimental.pallas import tpu as pltpu
from jax.sharding import PartitionSpec as P

HEAD_SIZE = 128
KEY_TILE = 256
CUT = 4
QUERY_TILE = 256
MASKED = -1e30
bf16 = jnp.bfloat16
f32 = jnp.float32
VMEM = pl.BlockSpec(memory_space=pltpu.VMEM)
SMEM = pl.BlockSpec(memory_space=pltpu.SMEM)
ANY = pl.BlockSpec(memory_space=pl.ANY)


def params(mib=14):
    return pltpu.CompilerParams(vmem_limit_bytes=mib * 2**20)


def cost(flops, moved, exps=0):
    return pl.CostEstimate(flops=flops, bytes_accessed=moved, transcendentals=exps)


def shape_of(shape, dtype):
    return jax.ShapeDtypeStruct(shape, dtype)


def pack_kernel(group, rows_ref, keys_hbm, values_hbm, queries_hbm, out_ref, queries_ref, sems):
    heads = out_ref.shape[0]
    frames = queries_ref.shape[0]
    per_head = rows_ref.shape[0] // heads
    copies = []
    for which, ref in enumerate((keys_hbm, values_hbm)):
        for g in range(heads):
            copies.append(
                pltpu.make_async_copy(
                    ref.at[:, pl.ds(g * HEAD_SIZE, HEAD_SIZE)],
                    out_ref.at[g, pl.ds(which * frames, frames), :],
                    sems.at[which * heads + g],
                )
            )
    pieces = []
    for p in range(4):
        span = pl.ds(p * (frames // 4), frames // 4)
        pieces.append(
            pltpu.make_async_copy(
                queries_hbm.at[span], queries_ref.at[span], sems.at[2 * heads + p]
            )
        )
    for copy in pieces + copies:
        copy.start()
    me = lax.axis_index("head")
    row = lax.broadcasted_iota(jnp.int32, (per_head, frames), 0)
    lane = lax.broadcasted_iota(jnp.int32, (per_head, frames), 1)
    wanted = jnp.full((per_head, frames), -1, jnp.int32)
    for i in range(per_head):
        wanted = jnp.where(row == i, rows_ref[me * per_head + i] - me * frames, wanted)
    chosen = jnp.where(lane == wanted, 1.0, 0.0).astype(bf16)
    for copy in pieces:
        copy.wait()
    picked = jnp.dot(chosen, queries_ref[...], preferred_element_type=f32)
    for g in range(heads):
        parts = [
            picked[:, (g * group + j) * HEAD_SIZE : (g * group + j + 1) * HEAD_SIZE]
            for j in range(group)
        ]
        out_ref[g, pl.ds(2 * frames, group * per_head), :] = jnp.concatenate(parts, axis=0).astype(
            bf16
        )
    for copy in copies:
        copy.wait()


def turned(row):
    return jnp.transpose(jnp.broadcast_to(row, (128, 128)))


def prep_kernel(
    group, rows_ref, ids_ref, owners_ref, targets_ref, docs_ref, told_ref, mine_ref, info_ref
):
    heads, frames = ids_ref.shape
    samples = rows_ref.shape[0]
    per_head = samples // heads
    docs = (ids_ref[...] + 1).astype(f32)
    docs_ref[...] = docs
    last = lax.axis_index("ctx") == lax.axis_size("ctx") - 1
    told_ref[...] = jnp.where(last, 0.0, docs)
    row = lax.broadcasted_iota(jnp.int32, (per_head, frames), 0)
    lane = lax.broadcasted_iota(jnp.int32, (per_head, frames), 1)
    for s in range(heads):
        place = jnp.zeros((per_head, frames), jnp.int32)
        for i in range(per_head):
            place = jnp.where(row == i, rows_ref[s * per_head + i] - s * frames, place)
        doc = jnp.sum(jnp.where(lane == place, docs[s : s + 1], 0.0), axis=1, keepdims=True)
        spot = ((heads + s) * frames + place).astype(f32)
        both = jnp.where(lane == 0, doc, spot)
        for j in range(group):
            mine_ref[pl.ds((s * group + j) * per_head, per_head), :] = both
    info_ref[...] = jnp.full(info_ref.shape, -1.0, f32)
    info_ref[0:1, 0:samples] = owners_ref[...].astype(f32)
    info_ref[2 : 2 + targets_ref.shape[0], 0:samples] = targets_ref[...].astype(f32)
    across = jnp.broadcast_to(info_ref[0:1, :], (128, 128))
    row = lax.broadcasted_iota(jnp.int32, (128, 128), 0)
    lane = lax.broadcasted_iota(jnp.int32, (128, 128), 1)
    same = (jnp.transpose(across) == across) & (row < lane)
    rank = jnp.sum(jnp.where(same, 1.0, 0.0), axis=0, keepdims=True)
    info_ref[1:2, :] = rank + (2 * lax.axis_index("ctx")).astype(f32)


def block_rows(s, own_ref, halo_ref, frames, which):
    heads = own_ref.shape[0]
    if s >= heads:
        return own_ref[s - heads, pl.ds(which * frames, frames), :]
    return halo_ref[pl.ds((2 * s + which) * frames, frames), :]


def window_kernel(before_ref, docs_ref, proj_hbm, all_docs_ref, low_ref, proj_ref, sem):
    fetch = pltpu.make_async_copy(proj_hbm, proj_ref, sem)
    fetch.start()
    docs = jnp.concatenate([before_ref[...], docs_ref[...]], axis=0)
    all_docs_ref[...] = docs
    for t in range(low_ref.shape[0]):
        first = docs_ref[t * QUERY_TILE // HEAD_SIZE : t * QUERY_TILE // HEAD_SIZE + 1, 0:1]
        below = jnp.where(docs < first, 1.0, 0.0)
        low_ref[t] = jnp.sum(below).astype(jnp.int32) // KEY_TILE
    fetch.wait()


def sample_kernel(
    scale,
    own_ref,
    halo_ref,
    before_ref,
    docs_ref,
    mine_ref,
    proj_ref,
    keep_ref,
    send_ref,
    scores_ref,
):
    heads = own_ref.shape[0]
    frames = docs_ref.shape[1]
    extra = own_ref.shape[1] - 2 * frames
    group = proj_ref.shape[0] // HEAD_SIZE
    per_head = extra // group
    rows = heads * extra
    tile = 2 * frames
    queries = own_ref[:, pl.ds(2 * frames, extra), :].reshape(rows, HEAD_SIZE)
    docs = jnp.concatenate([before_ref[...], docs_ref[...]], axis=0)
    my_doc = jnp.broadcast_to(mine_ref[:, 0:1], (rows, tile))
    my_place = jnp.broadcast_to(mine_ref[:, 1:2], (rows, tile))
    lane = lax.broadcasted_iota(jnp.int32, (rows, tile), 1).astype(f32)
    highest = jnp.full((rows, HEAD_SIZE), MASKED, f32)
    for s in range(0, 2 * heads, 2):
        key_tile = jnp.concatenate(
            [block_rows(s + i, own_ref, halo_ref, frames, 0) for i in range(2)], axis=0
        )
        scores = lax.dot_general(
            queries, key_tile, (((1,), (1,)), ((), ())), preferred_element_type=f32
        )
        tile_docs = jnp.concatenate([docs[s : s + 1], docs[s + 1 : s + 2]], axis=1)
        seen = (tile_docs == my_doc) & (lane <= my_place - s * frames)
        scores = jnp.where(seen, scores * scale, MASKED)
        start = s * frames
        scores_ref[:, start : start + tile] = scores
        for part in range(tile // HEAD_SIZE):
            highest = jnp.maximum(highest, scores[:, part * HEAD_SIZE : (part + 1) * HEAD_SIZE])
    top = jnp.max(highest, axis=1, keepdims=True)
    total = jnp.zeros((rows, HEAD_SIZE), f32)
    mixed = jnp.zeros((rows, HEAD_SIZE), f32)
    for s in range(0, 2 * heads, 2):
        value_tile = jnp.concatenate(
            [block_rows(s + i, own_ref, halo_ref, frames, 1) for i in range(2)], axis=0
        )
        start = s * frames
        weights = jnp.exp2(scores_ref[:, start : start + tile] - top)
        for part in range(tile // HEAD_SIZE):
            total = total + weights[:, part * HEAD_SIZE : (part + 1) * HEAD_SIZE]
        mixed = mixed + jnp.dot(weights.astype(bf16), value_tile, preferred_element_type=f32)
    attended = mixed / jnp.sum(total, axis=1, keepdims=True)
    by_group = attended.reshape(heads, group, per_head, HEAD_SIZE)
    state = jnp.zeros((heads * per_head, proj_ref.shape[1]), f32)
    for j in range(group):
        part = by_group[:, j].reshape(heads * per_head, HEAD_SIZE).astype(bf16)
        state = state + jnp.dot(
            part, proj_ref[pl.ds(j * HEAD_SIZE, HEAD_SIZE), :], preferred_element_type=f32
        )
    rows = state.shape[0] // 2
    odd = lax.rem(lax.axis_index("head"), 2) == 1
    keep_ref[...] = jnp.where(odd, state[rows:], state[:rows])
    send_ref[...] = jnp.where(odd, state[:rows], state[rows:]).astype(bf16)


def pair_kernel(keep_ref, came_ref, out_ref):
    state = (keep_ref[...] + came_ref[...].astype(f32)).astype(bf16)
    for d in range(out_ref.shape[0]):
        out_ref[d] = state


def logits_kernel(parts_ref, gain_ref, codes_ref, other_ref, info_ref, out_ref):
    count, samples, width = parts_ref.shape
    books, _, codes = codes_ref.shape
    me = lax.axis_index("head")
    odd = lax.rem(me, 2) == 1
    other = jnp.where(odd, me - 1, me + 1)
    info = info_ref[...]
    below = jnp.zeros((128 - info.shape[0], 128), f32)
    down = jnp.transpose(jnp.concatenate([info, below], axis=0))
    mine = jnp.where(odd, down[samples : 2 * samples], down[:samples])
    state = parts_ref[0].astype(f32)
    for s in range(1, count):
        state = state + parts_ref[s].astype(f32)
    square = jnp.sum(state * state, axis=1, keepdims=True)
    normed = (state * lax.rsqrt(square / width + 1e-06) * gain_ref[...]).astype(bf16)
    lane = lax.broadcasted_iota(jnp.int32, (samples, 128), 1)
    code = lax.broadcasted_iota(jnp.int32, (samples, codes), 1).astype(f32)
    stats = jnp.zeros((samples, 128), f32)
    for b in range(books):
        first = jnp.dot(normed, codes_ref[b], preferred_element_type=f32)
        second = jnp.dot(normed, other_ref[b], preferred_element_type=f32)
        top = jnp.max(jnp.maximum(first, second), axis=1, keepdims=True)
        mass = jnp.sum(jnp.exp(first - top) + jnp.exp(second - top), axis=1, keepdims=True)
        wanted = mine[:, 2 + b : 3 + b]
        hit = jnp.where(code == wanted - (me * codes).astype(f32), first, 0.0)
        hit = hit + jnp.where(code == wanted - (other * codes).astype(f32), second, 0.0)
        target = jnp.sum(hit, axis=1, keepdims=True)
        for k, figure in enumerate((top, mass, target)):
            stats = jnp.where(lane == 3 * b + k, figure, stats)
    none = jnp.zeros((samples, 128), f32)
    padded = jnp.concatenate(
        [jnp.where(odd, none, stats), jnp.where(odd, stats, none), none, none], axis=0
    )
    across = jnp.transpose(padded)[:8]
    for d in range(out_ref.shape[0]):
        out_ref[d] = across


def place_kernel(books, samples, stats_ref, info_ref, out_ref):
    heads = stats_ref.shape[0]
    losses = []
    for core in range(2):
        loss = jnp.zeros((1, 128), f32)
        for b in range(books):
            tops = [stats_ref[s, 3 * b : 3 * b + 1, :] for s in range(core, heads, 2)]
            top = functools.reduce(jnp.maximum, tops)
            mass = jnp.zeros((1, 128), f32)
            target = jnp.zeros((1, 128), f32)
            for i, s in enumerate(range(core, heads, 2)):
                mass = mass + stats_ref[s, 3 * b + 1 : 3 * b + 2, :] * jnp.exp(tops[i] - top)
                target = target + stats_ref[s, 3 * b + 2 : 3 * b + 3, :]
            loss = loss + (jnp.log(mass) + top - target)
        losses.append(loss * (1.0 / books))
    lane = lax.broadcasted_iota(jnp.int32, (1, 128), 1)
    loss = jnp.where(lane < samples // 2, losses[0], losses[1])
    contexts, slots = out_ref.shape
    owner = lax.broadcasted_iota(jnp.int32, (contexts, 128), 0).astype(f32)
    spread = jnp.where(info_ref[0:1, :] == owner, loss, 0.0)
    column = lax.broadcasted_iota(jnp.int32, (128, 128), 1).astype(f32)
    column = jnp.where(turned(info_ref[1:2, :]) == column, 1.0, 0.0)[:, :slots]
    out_ref[...] = jnp.dot(
        spread, column, preferred_element_type=f32, precision=lax.Precision.HIGHEST
    )


def main_kernel(scale, first_tile, steps, low_ref, queries_ref, own_ref, halo_ref, across_ref, *refs):
    out_ref, bias_ref, scores_ref, keys_ref, values_ref = refs[-5:]
    tile, width = queries_ref.shape
    group = width // HEAD_SIZE
    parts = tile // HEAD_SIZE
    block = keys_ref.shape[0] // 2
    number = first_tile + pl.program_id(0)
    start = block + number * tile
    low = low_ref[number]
    high = (start + tile + KEY_TILE - 1) // KEY_TILE
    halves = KEY_TILE // HEAD_SIZE
    units = [(j, r) for j in range(group) for r in range(parts)]
    frames = HEAD_SIZE
    sources = 2 * block // frames
    first_source = first_tile * parts
    last_source = sources // 2 + (first_tile + steps) * parts

    @pl.when(pl.program_id(0) == 0)
    def _():
        for s in range(first_source, last_source):
            rows = pl.ds(s * frames, frames)
            keys_ref[rows, :] = block_rows(s, own_ref, halo_ref, frames, 0)
            values_ref[rows, :] = block_rows(s, own_ref, halo_ref, frames, 1)


    def body(count):
        base = pl.multiple_of(low * KEY_TILE, KEY_TILE)
        ahead = lax.broadcasted_iota(jnp.int32, (HEAD_SIZE, HEAD_SIZE), 0) - lax.broadcasted_iota(
            jnp.int32, (HEAD_SIZE, HEAD_SIZE), 1
        )
        for r in range(parts):
            row = (block + number * tile) // HEAD_SIZE + r
            my_doc = turned(across_ref[pl.ds(row, 1), :])
            for k in range(count * halves):
                doc = across_ref[pl.ds(low * halves + k, 1), :]
                seen = (doc == my_doc) & (ahead >= base + k * HEAD_SIZE - start - r * HEAD_SIZE)
                bias_ref[r, :, k * HEAD_SIZE : (k + 1) * HEAD_SIZE] = jnp.where(seen, 0.0, MASKED)
        tops = []
        for u, (j, r) in enumerate(units):
            queries = queries_ref[r * HEAD_SIZE : (r + 1) * HEAD_SIZE, j * HEAD_SIZE : (j + 1) * HEAD_SIZE]
            highest = None
            for k in range(count):
                span = slice(k * KEY_TILE, (k + 1) * KEY_TILE)
                key_tile = keys_ref[pl.ds(base + k * KEY_TILE, KEY_TILE), :]
                scores = lax.dot_general(
                    queries, key_tile, (((1,), (1,)), ((), ())), preferred_element_type=f32
                )
                scores = scores * scale + bias_ref[r, :, span]
                scores_ref[u, :, span] = scores
                most = jnp.maximum(scores[:, :HEAD_SIZE], scores[:, HEAD_SIZE:])
                highest = most if highest is None else jnp.maximum(highest, most)
            tops.append(jnp.max(highest, axis=1, keepdims=True))
        one = jnp.ones((count * KEY_TILE, HEAD_SIZE), bf16)
        value_rows = jnp.concatenate([values_ref[pl.ds(base, count * KEY_TILE), :], one], axis=1)
        for u, (j, r) in enumerate(units):
            weights = jnp.concatenate(
                [
                    jnp.exp2(scores_ref[u, :, k * KEY_TILE : (k + 1) * KEY_TILE] - tops[u]).astype(bf16)
                    for k in range(count)
                ],
                axis=1,
            )
            mixed = jnp.dot(weights, value_rows, preferred_element_type=f32)
            out_ref[r * HEAD_SIZE : (r + 1) * HEAD_SIZE, j * HEAD_SIZE : (j + 1) * HEAD_SIZE] = (
                mixed[:, :HEAD_SIZE] / mixed[:, HEAD_SIZE:]
            ).astype(bf16)

    most = scores_ref.shape[2] // KEY_TILE
    for count in range(1, most + 1):
        pl.when(high - low == count)(functools.partial(body, count))


def attend(scale, first_tile, tiles, low, queries, own, halo, across, before):
    block, width = queries.shape
    tile = QUERY_TILE
    first_tile, tiles = first_tile * HEAD_SIZE // tile, tiles * HEAD_SIZE // tile
    group = width // HEAD_SIZE
    most = (block + tile + KEY_TILE - 1) // KEY_TILE
    rows = lambda i: (first_tile + i, 0)
    whole = lambda i: (0, 0)
    in_specs = [
        SMEM,
        pl.BlockSpec((tile, width), rows),
        pl.BlockSpec(own.shape, lambda i: (0, 0, 0)),
        pl.BlockSpec(halo.shape, whole),
        pl.BlockSpec(across.shape, whole),
    ]
    operands = [low, queries, own, halo, across]
    aliases = {}
    if before is not None:
        in_specs.append(pl.BlockSpec(memory_space=pl.ANY))
        operands.append(before)
        aliases = {len(operands) - 1: 0}
    pairs = tiles * group * tile * 4 * KEY_TILE
    return pl.pallas_call(
        functools.partial(main_kernel, scale, first_tile, tiles),
        grid=(tiles,),
        out_shape=shape_of((block, width), bf16),
        in_specs=in_specs,
        out_specs=pl.BlockSpec((tile, width), rows),
        scratch_shapes=[
            pltpu.VMEM((tile // HEAD_SIZE, HEAD_SIZE, most * KEY_TILE), f32),
            pltpu.VMEM((group * tile // HEAD_SIZE, HEAD_SIZE, most * KEY_TILE), f32),
            pltpu.VMEM((2 * block, HEAD_SIZE), bf16),
            pltpu.VMEM((2 * block, HEAD_SIZE), bf16),
        ],
        input_output_aliases=aliases,
        compiler_params=params(),
        cost_estimate=cost(pairs * 6 * HEAD_SIZE, 2 * 2**20, pairs),
    )(*operands)


def to_heads(value):
    return lax.all_to_all(value, "head", split_axis=0, concat_axis=0, tiled=True)


def after(value, *others):
    return lax.optimization_barrier((value, *others))[0]


def local(
    queries, keys, values, doc_ids, sample_rows, owners, targets, in_proj, dec_gain, code_heads
):
    heads = lax.axis_size("head")
    contexts = lax.axis_size("ctx")
    head_number = lax.axis_index("head")
    ctx_number = lax.axis_index("ctx")
    frames = keys.shape[0]
    block = doc_ids.shape[0]
    samples = sample_rows.shape[0]
    per_head = samples // heads
    width = queries.shape[1] // heads
    group = width // HEAD_SIZE
    scale = math.log2(math.e) / math.sqrt(HEAD_SIZE)
    deep = in_proj.shape[1]
    books = targets.shape[1]

    packed = pl.pallas_call(
        functools.partial(pack_kernel, group),
        out_shape=shape_of((heads, 2 * frames + group * per_head, HEAD_SIZE), bf16),
        in_specs=[SMEM, ANY, ANY, ANY],
        out_specs=VMEM,
        scratch_shapes=[
            pltpu.VMEM(queries.shape, bf16),
            pltpu.SemaphoreType.DMA((2 * heads + 4,)),
        ],
        compiler_params=params(56),
        cost_estimate=cost(2 * per_head * frames * queries.shape[1], 2 * 2**20),
    )(sample_rows, keys, values, queries)
    own = to_heads(packed)

    docs, told, mine, info = pl.pallas_call(
        functools.partial(prep_kernel, group),
        out_shape=(
            shape_of((heads, frames), f32),
            shape_of((heads, frames), f32),
            shape_of((samples * group, 128), f32),
            shape_of((8, 128), f32),
        ),
        in_specs=[SMEM, VMEM, VMEM, VMEM],
        out_specs=(VMEM,) * 4,
        compiler_params=params(8),
        cost_estimate=cost(10**6, 4 * 10**5),
    )(
        after(sample_rows, packed),
        doc_ids.reshape(heads, frames),
        owners.reshape(1, samples),
        targets.T,
    )
    ring = [(s, (s + 1) % contexts) for s in range(contexts)]
    before = lax.ppermute(told, "ctx", ring)
    by_head = jnp.transpose(after(queries, packed).reshape(frames, heads, width), (1, 0, 2))
    own, docs, mine, before, by_head = lax.optimization_barrier((own, docs, mine, before, by_head))
    halo = lax.ppermute(own[:, : 2 * frames].reshape(2 * block, HEAD_SIZE), "ctx", ring)
    queries_here = to_heads(by_head).reshape(block, width)
    pairs = [(s, s + 1 - 2 * (s % 2)) for s in range(heads)]
    other_codes = lax.ppermute(after(code_heads, own), "head", pairs)

    across, low, proj_here = pl.pallas_call(
        window_kernel,
        out_shape=(
            shape_of((2 * heads, frames), f32),
            shape_of((block // QUERY_TILE,), jnp.int32),
            shape_of(in_proj.shape, bf16),
        ),
        in_specs=[VMEM, VMEM, ANY],
        out_specs=(VMEM, SMEM, VMEM),
        scratch_shapes=[pltpu.SemaphoreType.DMA],
        compiler_params=params(8),
        cost_estimate=cost(0, 2 * 2**16),
    )(before, docs, after(in_proj, own))
    halo, across, low, proj_here = lax.optimization_barrier((halo, across, low, proj_here))
    keep, send = pl.pallas_call(
        functools.partial(sample_kernel, scale),
        out_shape=(shape_of((samples // 2, deep), f32), shape_of((samples // 2, deep), bf16)),
        in_specs=[VMEM] * 6,
        out_specs=(VMEM, VMEM),
        scratch_shapes=[pltpu.VMEM((samples * group, 2 * block), f32)],
        compiler_params=params(),
        cost_estimate=cost(
            240 * samples * group * 2 * block * HEAD_SIZE, 4 * 2**20, samples * group * 2 * block
        ),
    )(own, halo, before, docs, mine, proj_here)
    came = lax.ppermute(send, "head", pairs)

    shares = pl.pallas_call(
        pair_kernel,
        out_shape=shape_of((heads // 2, samples // 2, deep), bf16),
        in_specs=[VMEM] * 2,
        out_specs=VMEM,
        compiler_params=params(),
        cost_estimate=cost(samples * deep, 4 * samples * deep),
    )(keep, came)
    parts = lax.all_to_all(
        after(shares, queries_here),
        "head",
        split_axis=0,
        concat_axis=0,
        tiled=True,
        axis_index_groups=[list(range(core, heads, 2)) for core in range(2)],
    )
    tiles = block // HEAD_SIZE
    run = functools.partial(attend, scale)
    first_end = CUT
    attended = run(0, first_end, low, queries_here, own, halo, across, None)
    parts, attended = lax.optimization_barrier((parts, attended))
    codes_here = code_heads.shape[2]
    stats = pl.pallas_call(
        logits_kernel,
        out_shape=shape_of((heads, 8, 128), f32),
        in_specs=[VMEM] * 5,
        out_specs=VMEM,
        compiler_params=params(),
        cost_estimate=cost(4 * samples * deep * codes_here * books, code_heads.size * 4),
    )(parts, dec_gain[None, :], code_heads, other_codes, info)
    attended = run(
        first_end,
        tiles - first_end,
        after(low, stats),
        queries_here,
        own,
        halo,
        across,
        attended,
    )
    all_stats = to_heads(stats)

    all_stats, attended = lax.optimization_barrier((all_stats, attended))
    slot_count = 2 * contexts
    placed = pl.pallas_call(
        functools.partial(place_kernel, books, samples),
        out_shape=shape_of((contexts, slot_count), f32),
        in_specs=[VMEM] * 2,
        out_specs=VMEM,
        compiler_params=params(8),
        cost_estimate=cost(10**6, 10**5),
    )(all_stats, info)
    arrived = lax.all_to_all(placed, "ctx", split_axis=0, concat_axis=0, tiled=True)
    slot_loss = jnp.sum(arrived, axis=0, keepdims=True)
    return (attended, slot_loss)


def solution(mesh):
    in_specs = (
        P(("ctx", "head"), None),
        P(("ctx", "head"), None),
        P(("ctx", "head"), None),
        P("ctx"),
        P("ctx"),
        P("ctx", None),
        P("ctx", None),
        P("head", None),
        P(),
        P(None, None, "head"),
    )
    out_specs = (P("ctx", "head"), P("ctx", None))
    return jax.shard_map(local, mesh=mesh, in_specs=in_specs, out_specs=out_specs, check_vma=False)
```
